32 devices in a mesh: group: 8 (over z, x), tensor: 4 (over y, core).
Axes of the slice: x: 2, y: 2, z: 4, core: 2. Of those that a mesh axis runs over, the one named last changes fastest.
Arguments:
- tokens: bfloat16 [4096, 8192], P('group'), may hold values from -6 to 6
- norm_gain: float32 [8192], replicated, may hold values from 0.1 to 1.9
- w_key: bfloat16 [8192, 1024], P('group', 'tensor'), may hold values from -0.0625 to 0.0625
- w_value: bfloat16 [8192, 1024], P('group', 'tensor'), may hold values from -0.0625 to 0.0625
- positions: int32 [4096], P('group'), may hold values from 0 to 8191, as said below
- page_owner: int32 [256, 1], replicated, may hold values from 0 to 7; in each aligned block of 32 rows (0 to 31, 32 to 63, ...) at most 8 rows name the same one
- queries: bfloat16 [512, 8192], P('group', 'tensor'), may hold values from -100 to 100, as said below
- kv_cache: bfloat16 [512, 64, 2, 8, 128], P('group', None, None, 'tensor'), may hold values from -5 to 5
- cache_lengths: int32 [512], P('group'), may hold values from 2 to 64
Outputs:
- decoded: bfloat16 [512, 8192], P('group', 'tensor')
The draws below stay inside these ranges and needn't reach their ends.
Inputs may be any that keep to these rules, and one draw needn't show every extreme that they name: The queries are real values of order one or a few tens. Each page's tokens have consecutive positions. `page_owner`: at most 8 of one group index's pages go to one owner.
All inputs are finite; a program needn't handle non-finite values.
Results may differ from the reference program's by a relative error of at most 0.0054.
Values may be sent and summed in bfloat16 or wider, within the bound.
A program may use at most 192 MiB of HBM per device.

```python
import math
import jax
import jax.numpy as jnp
import numpy as np
from jax import lax

D = 8192
HEADS = 64
KVH = 8
HD = 128
PAGE = 16
CAP = 8
CACHE = 64
PAGES_DEV = 32
PAGES = 256
TOKENS = 4096
ROWS = 64
DEC_ROWS = 512
N_GROUP = 8


def first_keys(key):
    return jnp.clip(jax.random.normal(key, (DEC_ROWS, KVH, HD), jnp.float32), -5.0, 5.0)


def draw_kv_cache(key, part):
    leading = first_keys(key)
    key = jax.random.fold_in(key, 11)
    entries = jnp.clip(jax.random.normal(key, (DEC_ROWS, CACHE, 2, KVH, HD), jnp.float32), -5.0, 5.0)
    entries = entries.at[:, 0, 0].set(leading)
    return entries.astype(jnp.bfloat16)


def draw_queries(key, part):
    key = jax.random.fold_in(key, 12)
    base = jnp.clip(jax.random.normal(key, (DEC_ROWS, HEADS, HD), jnp.float32), -5.0, 5.0)
    return base.reshape(DEC_ROWS, HEADS * HD).astype(jnp.bfloat16)


def draw_positions(key, part):
    key = jax.random.fold_in(key, 13)
    starts = jax.random.randint(key, (TOKENS // PAGE,), 0, 512) * PAGE
    return (starts[:, None] + jnp.arange(PAGE)[None, :]).reshape(-1).astype(jnp.int32)


def place_ends(values, key, least, high):
    longest = values.shape.index(max(values.shape))
    spots = []
    for shift in (0, 1):
        where = [jax.random.randint(jax.random.fold_in(key, axis), (), 0, length) for axis, length in enumerate(values.shape)]
        where[longest] = (where[longest] + shift) % values.shape[longest]
        spots.append(tuple(where))
    return values.at[spots[0]].set(least).at[spots[1]].set(high)


def level_of(key, dims, split, smallest, largest):
    def one(dim, parts):
        heights = jax.random.uniform(jax.random.fold_in(jax.random.fold_in(key, 6), dim), (parts,), jnp.float32, smallest / len(split), largest / len(split))
        return jnp.repeat(jnp.exp(heights), dims[dim] // parts).reshape((-1,) + (1,) * (len(dims) - dim - 1))

    gain = one(*split[0])
    for cut in split[1:]:
        gain = gain * one(*cut)
    return gain


def shared_out(stream_key, own, number, rows, count, top, reach, lean):
    order = jax.random.permutation(stream_key, count)
    heavy_load, ordinary = portions_of(count, rows * top, reach, lean, True), portions_of(count, rows * top, reach, lean, False)
    places = jnp.arange(count)

    def named(sizes, rotation):
        used = int((sizes > 0).sum())
        fixed = max(1, used // 4)
        moved = fixed + (places - fixed + rotation * (used - fixed)) % max(1, count - fixed)
        return jnp.zeros((count,), jnp.int32).at[order[jnp.where(places < fixed, places, moved)]].set(jnp.asarray(sizes, jnp.int32))

    sizes = jnp.where(number % 4 == 0, named(heavy_load, number // 4), named(ordinary, number - number // 4 - 1))
    mixed = jax.random.permutation(jax.random.fold_in(own, 3), count)
    source_of, sink = mixed[0:count // 2 * 2:2], mixed[1:count // 2 * 2:2]
    margin = jnp.minimum(sizes[source_of] - 1, reach - sizes[sink]) // 2
    margin = jnp.where((source_of == order[0]) | (sink == order[0]) | (sizes[sink] == 0), 0, jnp.maximum(margin, 0))
    moved = jax.random.randint(jax.random.fold_in(own, 4), (count // 2,), 0, 1 << 20) % (margin + 1)
    sizes = sizes.at[source_of].add(-moved).at[sink].add(moved)
    labels = jnp.searchsorted(jnp.cumsum(sizes), jnp.arange(rows * top), side="right").astype(jnp.int32)
    grid = labels.reshape(top, rows).T
    grid = grid[jax.random.permutation(jax.random.fold_in(own, 1), rows)]
    rotation = jax.random.randint(jax.random.fold_in(own, 2), (rows, 1), 0, top)
    return jnp.take_along_axis(grid, (jnp.arange(top)[None, :] + rotation) % top, axis=1)


def portions_of(number_of, total, bound, slope, full):
    weights = [(1 << 20) // math.isqrt(grade ** slope) + 1 for grade in range(1, number_of + 1)]
    largest = bound if full else min(bound, max(-(-total // number_of), total * weights[0] // sum(weights)))
    least = 1 if total - largest >= number_of - 1 else 0
    holding, spare = [largest] + [least] * (number_of - 1), total - largest - least * (number_of - 1)
    while spare > 0:
        movable = [i for i in range(1, number_of) if holding[i] < largest] or [i for i in range(1, number_of) if holding[i] < bound]
        pool, left = sum([weights[i] for i in movable]), spare
        for i in movable:
            more = min(bound - holding[i], max(1, left * weights[i] // pool), spare)
            holding[i] = holding[i] + more
            spare = spare - more
    return np.array(holding)


def noise(own_key, dims, width, most, cuts=(), held_as=jnp.bfloat16):
    result = width * jax.random.normal(own_key, dims, jnp.float32)
    if cuts:
        result = result * level_of(own_key, dims, cuts, -0.22, 0.18)
    return jnp.clip(result, -most, most).astype(held_as)


def setup_inputs(seed: int = 0) -> dict:
    seeds = jax.random.split(jax.random.key(seed), 10)
    tokens = noise(seeds[0], (TOKENS, D), 1.0, 6.0, ((0, 8),))
    norm_gain = jnp.clip(1.0 + 0.18 * jax.random.normal(seeds[1], (D,), jnp.float32), 0.1, 1.9)
    w_key = noise(seeds[2], (D, KVH * HD), D ** -0.5, 0.0625, ((0, 8), (1, 4)))
    w_value = noise(seeds[3], (D, KVH * HD), D ** -0.5, 0.0625, ((0, 8), (1, 4)))
    positions = draw_positions(jax.random.fold_in(seeds[9], 71), 0)
    page_owner_keys = jax.random.split(jax.random.fold_in(seeds[5], 1), PAGES // PAGES_DEV)
    page_owner_turns = jax.random.permutation(jax.random.fold_in(seeds[5], 3), PAGES // PAGES_DEV)
    page_owner = jax.vmap(lambda own, number: shared_out(jax.random.fold_in(seeds[5], 2), own, number, PAGES_DEV, N_GROUP, 1, CAP, 1))(page_owner_keys, page_owner_turns).reshape((PAGES, 1))
    queries = draw_queries(jax.random.fold_in(seeds[9], 71), 0)
    kv_cache = draw_kv_cache(jax.random.fold_in(seeds[9], 71), 0)
    cache_lengths = place_ends(jax.random.randint(seeds[8], (DEC_ROWS,), 2, CACHE + 1), jax.random.fold_in(seeds[8], 1), 2, CACHE).astype(jnp.int32)
    return dict(tokens=tokens, norm_gain=norm_gain, w_key=w_key, w_value=w_value, positions=positions, page_owner=page_owner, queries=queries, kv_cache=kv_cache, cache_lengths=cache_lengths)


def rotate(keys, positions):
    half = keys.shape[-1] // 2
    index = jnp.arange(half).astype(jnp.float32)
    inverse = jnp.exp(index * (-2.0 * math.log(500000.0) / keys.shape[-1]))
    angles = positions.astype(jnp.float32)[:, None] * inverse[None, :]
    cosine = jnp.cos(angles)[:, None, :]
    sine = jnp.sin(angles)[:, None, :]
    first = keys[..., :half]
    second = keys[..., half:]
    return jnp.concatenate([first * cosine - second * sine, second * cosine + first * sine], -1)

def attend(queries, kv_cache, placed, filled, lengths):
    count = queries.shape[0]
    heads = kv_cache.shape[3]
    span = kv_cache.shape[1]
    query_f = queries.reshape(count, heads, -1, HD).astype(jnp.float32)
    scale = 1.0 / math.sqrt(HD)
    near = jnp.einsum('rhgd,rlhd->rhgl', query_f, kv_cache[:, :, 0].astype(jnp.float32)) * scale
    fresh = jnp.einsum('rhgd,rphd->rhgp', query_f, placed[:, :, 0].astype(jnp.float32)) * scale
    cache_ok = (jnp.arange(span)[None, :] < lengths[:, None])[:, None, None, :]
    page_ok = (filled > 0)[:, None, None, None]
    scores = jnp.concatenate([jnp.where(cache_ok, near, -1e+30), jnp.where(page_ok, fresh, -1e+30)], -1)
    top = lax.optimization_barrier(jnp.max(scores, -1, keepdims=True))
    weights = jnp.exp(scores - top)
    total = lax.optimization_barrier(jnp.sum(weights, -1, keepdims=True))
    probs = (weights / total).astype(jnp.bfloat16).astype(jnp.float32)
    output = jnp.einsum('rhgl,rlhd->rhgd', probs[..., :span], kv_cache[:, :, 1].astype(jnp.float32))
    output = output + jnp.einsum('rhgp,rphd->rhgd', probs[..., span:], placed[:, :, 1].astype(jnp.float32))
    return output.reshape(count, -1).astype(jnp.bfloat16)

def reference(tokens, norm_gain, w_key, w_value, positions, page_owner, queries, kv_cache, cache_lengths):
    values = tokens.astype(jnp.float32)
    factor = lax.rsqrt(lax.optimization_barrier(jnp.mean(values * values, -1, keepdims=True)) + 1e-05)
    normed = (values * factor * norm_gain[None, :]).astype(jnp.bfloat16)
    keys = jnp.dot(normed, w_key, preferred_element_type=jnp.float32).reshape(TOKENS, KVH, HD)
    keys = rotate(keys, positions).astype(jnp.bfloat16)
    vals = jnp.dot(normed, w_value, preferred_element_type=jnp.float32).astype(jnp.bfloat16).reshape(TOKENS, KVH, HD)
    page_kv = jnp.stack([keys, vals], 1).reshape(PAGES, PAGE, 2, KVH, HD)
    owner = page_owner[:, 0]
    source = (jnp.arange(PAGES) // PAGES_DEV).astype(jnp.int32)
    onehot = (owner[:, None] == jnp.arange(N_GROUP)[None, :]).astype(jnp.int32)
    blocked = onehot.reshape(N_GROUP, PAGES_DEV, N_GROUP)
    before = (jnp.cumsum(blocked, 1) - blocked).reshape(PAGES, N_GROUP)
    rank = lax.optimization_barrier(jnp.sum(before * onehot, 1)).astype(jnp.int32)
    target = (owner * ROWS + source * CAP + rank).astype(jnp.int32)
    placed = jnp.zeros((DEC_ROWS, PAGE, 2, KVH, HD), jnp.bfloat16).at[target].set(page_kv)
    filled = jnp.zeros((DEC_ROWS,), jnp.int32).at[target].set(1)

    def one_owner(items):
        return attend(*items)
    output = lax.map(one_owner, (queries.reshape(N_GROUP, ROWS, -1), kv_cache.reshape(N_GROUP, ROWS, CACHE, 2, KVH, HD), placed.reshape(N_GROUP, ROWS, PAGE, 2, KVH, HD), filled.reshape(N_GROUP, ROWS), cache_lengths.reshape(N_GROUP, ROWS)))
    return output.reshape(DEC_ROWS, HEADS * HD)
```

```python
import functools
import math

import jax
import jax.numpy as jnp
from jax import lax
from jax.experimental import pallas as pl
from jax.experimental.pallas import tpu as pltpu
from jax.sharding import PartitionSpec as P

HD = 128
PAGE = 16
CAP = 8


def rotate(keys, positions):
    half = keys.shape[-1] // 2
    index = jnp.arange(half).astype(jnp.float32)
    inverse = jnp.exp(index * (-2.0 * math.log(500000.0) / keys.shape[-1]))
    angles = positions.astype(jnp.float32)[:, None] * inverse[None, :]
    cosine = jnp.cos(angles)[:, None, :]
    sine = jnp.sin(angles)[:, None, :]
    first = keys[..., :half]
    second = keys[..., half:]
    return jnp.concatenate([first * cosine - second * sine, second * cosine + first * sine], -1)


def attend(queries, kv_cache, placed, filled, lengths):
    count = queries.shape[0]
    heads = kv_cache.shape[3]
    span = kv_cache.shape[1]
    query_b = queries.reshape(count, heads, -1, HD)
    scale = 1.0 / math.sqrt(HD)
    near = (
        jnp.einsum(
            "rhgd,rlhd->rhgl", query_b, kv_cache[:, :, 0], preferred_element_type=jnp.float32
        )
        * scale
    )
    fresh = (
        jnp.einsum("rhgd,rphd->rhgp", query_b, placed[:, :, 0], preferred_element_type=jnp.float32)
        * scale
    )
    cache_ok = (jnp.arange(span)[None, :] < lengths[:, None])[:, None, None, :]
    page_ok = (filled > 0)[:, None, None, None]
    scores = jnp.concatenate(
        [jnp.where(cache_ok, near, -1e30), jnp.where(page_ok, fresh, -1e30)], -1
    )
    top = jnp.max(scores, -1, keepdims=True)
    weights = jnp.exp(scores - top)
    total = jnp.sum(weights, -1, keepdims=True)
    probs = (weights / total).astype(jnp.bfloat16)
    output = jnp.einsum(
        "rhgl,rlhd->rhgd", probs[..., :span], kv_cache[:, :, 1], preferred_element_type=jnp.float32
    )
    output = output + jnp.einsum(
        "rhgp,rphd->rhgd", probs[..., span:], placed[:, :, 1], preferred_element_type=jnp.float32
    )
    return output.reshape(count, -1).astype(jnp.bfloat16)


def per_device(
    tokens, norm_gain, w_key, w_value, positions, page_owner, queries, kv_cache, cache_lengths
):
    tok_count = tokens.shape[0]
    values = tokens.astype(jnp.float32)
    factor = lax.rsqrt(jnp.mean(values * values, -1, keepdims=True) + 1e-05)
    normed = (values * factor * norm_gain[None, :]).astype(jnp.bfloat16)
    full_key, full_value = (
        lax.all_gather(w_key, "group", axis=0, tiled=True),
        lax.all_gather(w_value, "group", axis=0, tiled=True),
    )
    key_sum = jnp.dot(normed, full_key, preferred_element_type=jnp.float32)
    value_sum = jnp.dot(normed, full_value, preferred_element_type=jnp.float32)
    heads = w_key.shape[1] // HD
    keys = rotate(key_sum.reshape(tok_count, heads, HD), positions).astype(jnp.bfloat16)
    vals = value_sum.astype(jnp.bfloat16).reshape(tok_count, heads, HD)
    pages = tok_count // PAGE
    page_kv = jnp.stack([keys, vals], 1).reshape(pages, PAGE * 2 * heads * HD)
    ngroup = lax.axis_size("group")
    myself = lax.axis_index("group")
    owners_all = page_owner[:, 0].reshape(ngroup, pages)
    owned = lax.dynamic_index_in_dim(owners_all, myself, 0, keepdims=False)
    onehot = (owned[:, None] == jnp.arange(ngroup)[None, :]).astype(jnp.float32)
    earlier = (jnp.arange(pages)[:, None] > jnp.arange(pages)[None, :]).astype(jnp.float32)
    before = jnp.dot(earlier, onehot, preferred_element_type=jnp.float32)
    rank = jnp.sum(before * onehot, 1).astype(jnp.int32)
    target = owned * CAP + rank
    chooser = (jnp.arange(ngroup * CAP)[:, None] == target[None, :]).astype(jnp.bfloat16)
    outgoing = jnp.dot(chooser, page_kv, preferred_element_type=jnp.float32).astype(jnp.bfloat16)
    outgoing = outgoing.reshape(ngroup * CAP, PAGE, 2, heads, HD)
    received = lax.all_to_all(outgoing, "group", split_axis=0, concat_axis=0, tiled=True)
    counts = jnp.sum((owners_all == myself).astype(jnp.int32), 1)
    filled = (jnp.arange(CAP)[None, :] < counts[:, None]).reshape(-1).astype(jnp.int32)
    return attend(queries, kv_cache, received, filled, cache_lengths)


MESH = pl.DeviceIdType.MESH
VMEM_BUDGET = 56 * 2**20


def project_kernel(
    n_group,
    n_tensor,
    cut,
    tok_ref,
    gain_ref,
    wk_ref,
    wv_ref,
    cos_ref,
    sin_ref,
    target_ref,
    out_ref,
    tok,
    wbuf,
    acc,
    choose,
    obuf,
    tok_sem,
    own_sem,
    up_sem,
    down_sem,
    main_sem,
    tail_up_sem,
    tail_down_sem,
    tail_sem,
    xhead_send,
    xtail_send,
    xhead_sem,
    page_send,
    page_recv,
):
    line = n_group // 2
    depth, cols = wk_ref.shape
    count = tok.shape[0]
    me = lax.axis_index("group")
    mine = lax.axis_index("tensor")
    z = lax.div(me, 2)
    x = lax.rem(me, 2)
    peer_x = 1 - x
    peer = z * 2 + peer_x
    head_rows = pl.ds(0, cut)
    tail_rows = pl.ds(cut, depth - cut)

    def send(src, dst, send_sem, recv_sem, group):
        return pltpu.make_async_remote_copy(
            src_ref=src,
            dst_ref=dst,
            send_sem=send_sem,
            recv_sem=recv_sem,
            device_id=(group, mine),
            device_id_type=MESH,
        )

    def block(ph, zz, xx):
        return wbuf.at[ph, zz * 2 + xx]

    def main_copy(ph, zz, up, src=None):
        src = block(ph, zz, x) if src is None else src
        sem, to = (up_sem, me + 2) if up else (down_sem, me - 2)
        return send(src, block(ph, zz, x), sem.at[ph, zz], main_sem.at[ph, zz], to)

    def tail_copy(ph, zz, up):
        part = wbuf.at[ph, zz * 2 + peer_x, tail_rows]
        sem, to = (tail_up_sem, me + 2) if up else (tail_down_sem, me - 2)
        return send(part, part, sem.at[ph, zz], tail_sem.at[ph, zz], to)

    def xhead_copy(ph, zz, column):
        part = wbuf.at[ph, zz * 2 + column, head_rows]
        return send(part, part, xhead_send.at[ph, zz], xhead_sem.at[ph, zz], peer)

    def xtail_copy(ph, column):
        part = wbuf.at[ph, z * 2 + column, tail_rows]
        return send(part, part, xtail_send.at[ph], tail_sem.at[ph, z], peer)

    def both_ways(make):
        @pl.when(z < line - 1)
        def _():
            make(True)

        @pl.when(z > 0)
        def _():
            make(False)

    weights = (wv_ref, wk_ref)

    def own_load(ph):
        return pltpu.make_async_copy(weights[ph], wbuf.at[ph, me], own_sem.at[ph])

    def start_own(ph):
        both_ways(lambda up: main_copy(ph, z, up).start())
        xtail_copy(ph, x).start()
        xhead_copy(ph, z, x).start()

    def pass_own_tail(ph):
        xtail_copy(ph, peer_x).wait_recv()
        both_ways(lambda up: tail_copy(ph, z, up).start())

    own_load(0).start()
    own_load(1).start()
    tok_load = pltpu.make_async_copy(tok_ref, tok, tok_sem)
    tok_load.start()

    barrier = pltpu.get_barrier_semaphore()
    for step in range(1, n_group):
        pl.semaphore_signal(
            barrier,
            inc=1,
            device_id=(lax.rem(me + step, n_group), mine),
            device_id_type=MESH,
        )
    pl.semaphore_wait(barrier, n_group - 1)

    own_load(0).wait()
    start_own(0)
    acc[...] = jnp.zeros_like(acc)
    own_load(1).wait()
    tok_load.wait()

    chunk = 32
    width = tok.shape[1]
    piece = 1024

    @pl.loop(0, count // chunk)
    def _(i):
        rows = pl.ds(pl.multiple_of(i * chunk, chunk), chunk)
        total = jnp.zeros((chunk, 128), jnp.float32)
        for k in range(width // piece):
            part = tok[rows, k * piece : (k + 1) * piece].astype(jnp.float32)
            part = part * part
            for j in range(piece // 128):
                total = total + part[:, j * 128 : (j + 1) * 128]
        mean = jnp.sum(total, -1, keepdims=True) * (1.0 / width)
        factor = lax.rsqrt(mean + 1e-05)
        for k in range(width // piece):
            span = slice(k * piece, (k + 1) * piece)
            part = tok[rows, span].astype(jnp.float32) * factor * gain_ref[:, span]
            tok[rows, span] = part.astype(jnp.bfloat16)

    pass_own_tail(0)

    slots = choose.shape[0]

    @pl.loop(0, slots // 128)
    def _(i):
        start = pl.multiple_of(i * 128, 128)
        row = lax.broadcasted_iota(jnp.int32, (128, count), 0) + start
        hit = row == target_ref[...]
        choose[pl.ds(start, 128), :] = jnp.where(hit, 1.0, 0.0).astype(jnp.bfloat16)

    half = count // 2

    def multiply(ph, index):
        span = pl.ds(pl.multiple_of(index * depth, depth), depth)

        @pl.loop(0, 2)
        def _(i):
            rows = pl.ds(pl.multiple_of(i * half, half), half)
            acc[ph, rows, :] += jnp.dot(
                tok[rows, span], wbuf[ph, index], preferred_element_type=jnp.float32
            )

    per_owner = slots // n_group

    def page_copy(ph, step):
        to = lax.rem(me + step, n_group)
        return send(
            obuf.at[ph, to], out_ref.at[ph, me], page_send.at[ph, to], page_recv.at[ph, me], to
        )

    def page_wait(ph, step):
        origin = lax.rem(me + step, n_group)
        send(
            obuf.at[ph, origin],
            out_ref.at[ph, origin],
            page_send.at[ph, origin],
            page_recv.at[ph, origin],
            origin,
        ).wait_recv()

    def hand_over(ph):
        held = acc[ph]
        if ph == 1:
            turned = [
                held[:, s : s + HD] * cos_ref[...]
                + pltpu.roll(held[:, s : s + HD], HD // 2, 1) * sin_ref[...]
                for s in range(0, cols, HD)
            ]
            held = jnp.concatenate(turned, -1)
        held = held.astype(jnp.bfloat16)

        for owner in range(n_group):
            rows = choose[owner * per_owner : (owner + 1) * per_owner, :]
            picked = jnp.dot(rows, held, preferred_element_type=jnp.float32)
            obuf[ph, owner] = picked.astype(jnp.bfloat16)
        for step in range(1, n_group):
            page_copy(ph, step).start()
        out_ref[ph, me] = obuf[ph, me]

    def at(step, way):
        ph = lax.div(step, line)
        dist = lax.rem(step, line)
        zz = z + dist * (2 * way - 1)
        live = (zz >= 0) & (zz < line) & ((dist > 0) | (way == 0))
        return ph, dist, zz, live

    def forward(ph, dist, zz, way, copy):
        @pl.when((way == 0) & (z < line - 1))
        def _():
            copy(ph, zz, True).start()

        @pl.when((way == 1) & (z > 0))
        def _():
            copy(ph, zz, False).start()

    @pl.loop(0, 2 * line + 1)
    def _(step):
        @pl.when(step < 2 * line)
        def _():
            @pl.loop(0, 2)
            def _(way):
                ph, dist, zz, live = at(step, way)

                @pl.when(live & (dist > 0))
                def _():
                    main_copy(ph, zz, True).wait_recv()
                    forward(ph, dist, zz, way, main_copy)
                    xhead_copy(ph, zz, x).start()

            @pl.loop(0, 2)
            def _(way):
                ph, dist, zz, live = at(step, way)

                @pl.when(live & (dist > 0))
                def _():
                    tail_copy(ph, zz, True).wait_recv()
                    forward(ph, dist, zz, way, tail_copy)

            @pl.when(step == 1)
            def _():
                start_own(1)

            @pl.when(step == 2)
            def _():
                pass_own_tail(1)

            @pl.loop(0, 2)
            def _(way):
                ph, dist, zz, live = at(step, way)

                @pl.when(live)
                def _():
                    multiply(ph, zz * 2 + x)

        @pl.when(step > 0)
        def _():
            @pl.loop(0, 2)
            def _(way):
                ph, dist, zz, live = at(step - 1, way)

                @pl.when(live)
                def _():
                    xhead_copy(ph, zz, peer_x).wait_recv()
                    multiply(ph, zz * 2 + peer_x)

        @pl.when(step == line)
        def _():
            hand_over(0)

    hand_over(1)

    for ph in range(2):
        xtail_copy(ph, x).wait_send()
        for zz in range(line):
            xhead_copy(ph, zz, x).wait_send()

            @pl.when((z < line - 1) & (zz <= z))
            def _():
                main_copy(ph, zz, True).wait_send()
                tail_copy(ph, zz, True).wait_send()

            @pl.when((z > 0) & (zz >= z))
            def _():
                main_copy(ph, zz, False).wait_send()
                tail_copy(ph, zz, False).wait_send()

        for step in range(1, n_group):
            page_copy(ph, step).wait_send()
            page_wait(ph, step)


def project(n_group, n_tensor, tokens, norm_gain, w_key, w_value, cosine, sine, target):
    count, width = tokens.shape
    depth, cols = w_key.shape
    line = n_group // 2
    slots = n_group * CAP * PAGE
    cut = depth - depth // 8
    vmem = pl.BlockSpec(memory_space=pltpu.VMEM)
    hbm = pl.BlockSpec(memory_space=pl.ANY)
    dma = pltpu.SemaphoreType.DMA
    return pl.pallas_call(
        functools.partial(project_kernel, n_group, n_tensor, cut),
        out_shape=jax.ShapeDtypeStruct((2, n_group, slots // n_group, cols), jnp.bfloat16),
        in_specs=[hbm, vmem, hbm, hbm, vmem, vmem, vmem],
        out_specs=vmem,
        scratch_shapes=[
            pltpu.VMEM((count, width), jnp.bfloat16),
            pltpu.VMEM((2, n_group, depth, cols), jnp.bfloat16),
            pltpu.VMEM((2, count, cols), jnp.float32),
            pltpu.VMEM((slots, count), jnp.bfloat16),
            pltpu.VMEM((2, n_group, slots // n_group, cols), jnp.bfloat16),
            dma,
            dma((2,)),
            dma((2, line)),
            dma((2, line)),
            dma((2, line)),
            dma((2, line)),
            dma((2, line)),
            dma((2, line)),
            dma((2, line)),
            dma((2,)),
            dma((2, line)),
            dma((2, n_group)),
            dma((2, n_group)),
        ],
        compiler_params=pltpu.CompilerParams(
            collective_id=0, has_side_effects=True, vmem_limit_bytes=VMEM_BUDGET
        ),
        cost_estimate=pl.CostEstimate(
            flops=4 * count * width * cols,
            bytes_accessed=2 * count * width + 4 * depth * cols,
            transcendentals=0,
        ),
    )(tokens, norm_gain[None, :], w_key, w_value, cosine, sine, target)


def page_targets(page_owner, ngroup, pages, myself):
    owners_all = page_owner[:, 0].reshape(ngroup, pages)
    owned = lax.dynamic_index_in_dim(owners_all, myself, 0, keepdims=False)
    earlier = jnp.arange(pages)[:, None] > jnp.arange(pages)[None, :]
    same = owned[:, None] == owned[None, :]
    rank = jnp.sum((earlier & same).astype(jnp.int32), 1)
    counts = jnp.sum((owners_all == myself).astype(jnp.int32), 1)
    filled = (jnp.arange(CAP)[None, :] < counts[:, None]).reshape(-1).astype(jnp.int32)
    return owned * CAP + rank, filled


def per_device_fused(
    tokens, norm_gain, w_key, w_value, positions, page_owner, queries, kv_cache, cache_lengths
):
    count = tokens.shape[0]
    pages = count // PAGE
    ngroup = lax.axis_size("group")
    ntensor = lax.axis_size("tensor")
    myself = lax.axis_index("group")
    index = jnp.arange(HD // 2).astype(jnp.float32)
    inverse = jnp.exp(index * (-2.0 * math.log(500000.0) / HD))
    angles = positions.astype(jnp.float32)[:, None] * inverse[None, :]
    cosine, sine = jnp.cos(angles), jnp.sin(angles)
    cosine = jnp.concatenate([cosine, cosine], -1)
    sine = jnp.concatenate([-sine, sine], -1)
    target, filled = page_targets(page_owner, ngroup, pages, myself)
    rows = (target[:, None] * PAGE + jnp.arange(PAGE)[None, :]).reshape(1, count)
    placed = project(
        ngroup, ntensor, tokens, norm_gain, w_key, w_value, cosine, sine, rows
    )
    heads = w_key.shape[1] // HD
    placed = placed.reshape(2, ngroup * CAP, PAGE, heads, HD)
    received = jnp.stack([placed[1], placed[0]], 2)
    return attend(queries, kv_cache, received, filled, cache_lengths)


def fits(count, width, cols, ngroup):
    slots = ngroup * CAP * PAGE
    held = 2 * count * width + 4 * width * cols + 8 * count * cols
    held += 2 * slots * count + 8 * slots * cols + 8 * count * HD
    return 3 * held < 2 * VMEM_BUDGET


def pick(tokens, norm_gain, w_key, *rest):
    ngroup = lax.axis_size("group")
    count, width = tokens.shape
    fused = ngroup % 2 == 0 and count % 256 == 0 and w_key.shape[0] % 1024 == 0
    fused = fused and fits(count, width, w_key.shape[1], ngroup)
    return (per_device_fused if fused else per_device)(tokens, norm_gain, w_key, *rest)


def solution(mesh):
    return jax.shard_map(
        pick,
        mesh=mesh,
        in_specs=(
            P("group", None),
            P(),
            P("group", "tensor"),
            P("group", "tensor"),
            P("group"),
            P(),
            P("group", "tensor"),
            P("group", None, None, "tensor", None),
            P("group"),
        ),
        out_specs=P("group", "tensor"),
        check_vma=False,
    )
```

```python
import functools
import math

import jax
import jax.numpy as jnp
from jax import lax
from jax.experimental import pallas as pl
from jax.experimental.pallas import tpu as pltpu
from jax.sharding import PartitionSpec as P

HD = 128
PAGE = 16
CAP = 8


def rotate(keys, positions):
    half = keys.shape[-1] // 2
    index = jnp.arange(half).astype(jnp.float32)
    inverse = jnp.exp(index * (-2.0 * math.log(500000.0) / keys.shape[-1]))
    angles = positions.astype(jnp.float32)[:, None] * inverse[None, :]
    cosine = jnp.cos(angles)[:, None, :]
    sine = jnp.sin(angles)[:, None, :]
    first = keys[..., :half]
    second = keys[..., half:]
    return jnp.concatenate([first * cosine - second * sine, second * cosine + first * sine], -1)


def attend(queries, kv_cache, placed, filled, lengths):
    count = queries.shape[0]
    heads = kv_cache.shape[3]
    span = kv_cache.shape[1]
    query_b = queries.reshape(count, heads, -1, HD)
    scale = 1.0 / math.sqrt(HD)
    near = (
        jnp.einsum(
            "rhgd,rlhd->rhgl", query_b, kv_cache[:, :, 0], preferred_element_type=jnp.float32
        )
        * scale
    )
    fresh = (
        jnp.einsum("rhgd,rphd->rhgp", query_b, placed[:, :, 0], preferred_element_type=jnp.float32)
        * scale
    )
    cache_ok = (jnp.arange(span)[None, :] < lengths[:, None])[:, None, None, :]
    page_ok = (filled > 0)[:, None, None, None]
    scores = jnp.concatenate(
        [jnp.where(cache_ok, near, -1e30), jnp.where(page_ok, fresh, -1e30)], -1
    )
    top = jnp.max(scores, -1, keepdims=True)
    weights = jnp.exp(scores - top)
    total = jnp.sum(weights, -1, keepdims=True)
    probs = (weights / total).astype(jnp.bfloat16)
    output = jnp.einsum(
        "rhgl,rlhd->rhgd", probs[..., :span], kv_cache[:, :, 1], preferred_element_type=jnp.float32
    )
    output = output + jnp.einsum(
        "rhgp,rphd->rhgd", probs[..., span:], placed[:, :, 1], preferred_element_type=jnp.float32
    )
    return output.reshape(count, -1).astype(jnp.bfloat16)


def per_device(
    tokens, norm_gain, w_key, w_value, positions, page_owner, queries, kv_cache, cache_lengths
):
    tok_count = tokens.shape[0]
    values = tokens.astype(jnp.float32)
    factor = lax.rsqrt(jnp.mean(values * values, -1, keepdims=True) + 1e-05)
    normed = (values * factor * norm_gain[None, :]).astype(jnp.bfloat16)
    full_key, full_value = (
        lax.all_gather(w_key, "group", axis=0, tiled=True),
        lax.all_gather(w_value, "group", axis=0, tiled=True),
    )
    key_sum = jnp.dot(normed, full_key, preferred_element_type=jnp.float32)
    value_sum = jnp.dot(normed, full_value, preferred_element_type=jnp.float32)
    heads = w_key.shape[1] // HD
    keys = rotate(key_sum.reshape(tok_count, heads, HD), positions).astype(jnp.bfloat16)
    vals = value_sum.astype(jnp.bfloat16).reshape(tok_count, heads, HD)
    pages = tok_count // PAGE
    page_kv = jnp.stack([keys, vals], 1).reshape(pages, PAGE * 2 * heads * HD)
    ngroup = lax.axis_size("group")
    myself = lax.axis_index("group")
    owners_all = page_owner[:, 0].reshape(ngroup, pages)
    owned = lax.dynamic_index_in_dim(owners_all, myself, 0, keepdims=False)
    onehot = (owned[:, None] == jnp.arange(ngroup)[None, :]).astype(jnp.float32)
    earlier = (jnp.arange(pages)[:, None] > jnp.arange(pages)[None, :]).astype(jnp.float32)
    before = jnp.dot(earlier, onehot, preferred_element_type=jnp.float32)
    rank = jnp.sum(before * onehot, 1).astype(jnp.int32)
    target = owned * CAP + rank
    chooser = (jnp.arange(ngroup * CAP)[:, None] == target[None, :]).astype(jnp.bfloat16)
    outgoing = jnp.dot(chooser, page_kv, preferred_element_type=jnp.float32).astype(jnp.bfloat16)
    outgoing = outgoing.reshape(ngroup * CAP, PAGE, 2, heads, HD)
    received = lax.all_to_all(outgoing, "group", split_axis=0, concat_axis=0, tiled=True)
    counts = jnp.sum((owners_all == myself).astype(jnp.int32), 1)
    filled = (jnp.arange(CAP)[None, :] < counts[:, None]).reshape(-1).astype(jnp.int32)
    return attend(queries, kv_cache, received, filled, cache_lengths)


MESH = pl.DeviceIdType.MESH
VMEM_BUDGET = 56 * 2**20


def project_kernel(
    n_group,
    cut,
    tok_ref,
    gain_ref,
    wk_ref,
    wv_ref,
    pos_ref,
    owner_ref,
    query_ref,
    cache_ref,
    length_ref,
    out_ref,
    tok,
    wbuf,
    acc,
    choose,
    obuf,
    rbuf,
    cos_ref,
    sin_ref,
    cache,
    query_f,
    query_b,
    near_out,
    near_max,
    near_sum,
    result,
    tok_sem,
    cache_sem,
    own_sem,
    up_sem,
    down_sem,
    main_sem,
    tail_up_sem,
    tail_down_sem,
    tail_sem,
    xhead_send,
    xtail_send,
    xhead_sem,
    page_send,
    page_recv,
):
    line = n_group // 2
    depth, cols = wk_ref.shape
    count = tok.shape[0]
    me = lax.axis_index("group")
    mine = lax.axis_index("tensor")
    z = lax.div(me, 2)
    x = lax.rem(me, 2)
    peer_x = 1 - x
    peer = z * 2 + peer_x
    head_rows = pl.ds(0, cut)
    tail_rows = pl.ds(cut, depth - cut)

    def send(src, dst, send_sem, recv_sem, group):
        return pltpu.make_async_remote_copy(
            src_ref=src,
            dst_ref=dst,
            send_sem=send_sem,
            recv_sem=recv_sem,
            device_id=(group, mine),
            device_id_type=MESH,
        )

    def block(ph, zz, xx):
        return wbuf.at[ph, zz * 2 + xx]

    def main_copy(ph, zz, up, src=None):
        src = block(ph, zz, x) if src is None else src
        sem, to = (up_sem, me + 2) if up else (down_sem, me - 2)
        return send(src, block(ph, zz, x), sem.at[ph, zz], main_sem.at[ph, zz], to)

    def tail_copy(ph, zz, up):
        part = wbuf.at[ph, zz * 2 + peer_x, tail_rows]
        sem, to = (tail_up_sem, me + 2) if up else (tail_down_sem, me - 2)
        return send(part, part, sem.at[ph, zz], tail_sem.at[ph, zz], to)

    def xhead_copy(ph, zz, column):
        part = wbuf.at[ph, zz * 2 + column, head_rows]
        return send(part, part, xhead_send.at[ph, zz], xhead_sem.at[ph, zz], peer)

    def xtail_copy(ph, column):
        part = wbuf.at[ph, z * 2 + column, tail_rows]
        return send(part, part, xtail_send.at[ph], tail_sem.at[ph, z], peer)

    def both_ways(make):
        @pl.when(z < line - 1)
        def _():
            make(True)

        @pl.when(z > 0)
        def _():
            make(False)

    weights = (wv_ref, wk_ref)

    def own_load(ph):
        return pltpu.make_async_copy(weights[ph], wbuf.at[ph, me], own_sem.at[ph])

    def start_own(ph):
        both_ways(lambda up: main_copy(ph, z, up).start())
        xtail_copy(ph, x).start()
        xhead_copy(ph, z, x).start()

    def pass_own_tail(ph):
        xtail_copy(ph, peer_x).wait_recv()
        both_ways(lambda up: tail_copy(ph, z, up).start())

    own_load(0).start()
    own_load(1).start()
    tok_load = pltpu.make_async_copy(tok_ref, tok, tok_sem)
    tok_load.start()
    cache_load = pltpu.make_async_copy(cache_ref, cache, cache_sem)
    cache_load.start()

    barrier = pltpu.get_barrier_semaphore()
    for step in range(1, n_group):
        pl.semaphore_signal(
            barrier,
            inc=1,
            device_id=(lax.rem(me + step, n_group), mine),
            device_id_type=MESH,
        )
    pl.semaphore_wait(barrier, n_group - 1)

    own_load(0).wait()
    start_own(0)
    acc[...] = jnp.zeros_like(acc)
    own_load(1).wait()
    tok_load.wait()

    chunk = 32
    width = tok.shape[1]
    piece = 1024

    @pl.loop(0, count // chunk)
    def _(i):
        rows = pl.ds(pl.multiple_of(i * chunk, chunk), chunk)
        total = jnp.zeros((chunk, 128), jnp.float32)
        for k in range(width // piece):
            part = tok[rows, k * piece : (k + 1) * piece].astype(jnp.float32)
            part = part * part
            for j in range(piece // 128):
                total = total + part[:, j * 128 : (j + 1) * 128]
        mean = jnp.sum(total, -1, keepdims=True) * (1.0 / width)
        factor = lax.rsqrt(mean + 1e-05)
        for k in range(width // piece):
            span = slice(k * piece, (k + 1) * piece)
            part = tok[rows, span].astype(jnp.float32) * factor * gain_ref[:, span]
            tok[rows, span] = part.astype(jnp.bfloat16)

    pass_own_tail(0)

    slots = choose.shape[0]
    owned_pages = count // PAGE
    every = owner_ref.shape[1]

    def grid_of(shape, dim):
        return lax.broadcasted_iota(jnp.int32, shape, dim)

    def column(row):
        size = row.shape[1]
        same = grid_of((size, size), 0) == grid_of((size, size), 1)
        return jnp.sum(jnp.where(same, row, 0), 1, keepdims=True)

    owner_row = owner_ref[...].astype(jnp.float32)
    owner_col = column(owner_row)
    first = grid_of((every, every), 0)
    second = grid_of((every, every), 1)
    before = (owner_col == owner_row) & (first < second)
    before = before & (first // owned_pages == second // owned_pages)
    rank = jnp.sum(jnp.where(before, 1.0, 0.0), 0, keepdims=True)
    place = owner_row * CAP + rank
    page_of = grid_of((every, count), 0) == me * owned_pages + grid_of((every, count), 1) // PAGE
    place_col = column(place)
    token_place = jnp.sum(jnp.where(page_of, place_col, 0.0), 0, keepdims=True)
    token_row = token_place.astype(jnp.int32) * PAGE + grid_of((1, count), 1) % PAGE

    lane = grid_of((1, HD), 1)
    index = (lane % (HD // 2)).astype(jnp.float32)
    inverse = jnp.exp(index * (-2.0 * math.log(500000.0) / HD))
    for start in range(0, count, 128):
        angles = column(pos_ref[:, start : start + 128].astype(jnp.float32)) * inverse
        cos_ref[start : start + 128, :] = jnp.cos(angles)
        turn = jnp.sin(angles)
        sin_ref[start : start + 128, :] = jnp.where(lane < HD // 2, -turn, turn)

    @pl.loop(0, slots // 128)
    def _(i):
        start = pl.multiple_of(i * 128, 128)
        row = lax.broadcasted_iota(jnp.int32, (128, count), 0) + start
        hit = row == token_row
        choose[pl.ds(start, 128), :] = jnp.where(hit, 1.0, 0.0).astype(jnp.bfloat16)

    query_f[...] = query_ref[...].astype(jnp.float32)
    heads = query_f.shape[1] // HD
    kv_heads = cols // HD
    share = heads // kv_heads
    group_rows = heads * CAP
    span_rows = cache.shape[0] // n_group
    live_span = span_rows // (CAP * 2 * kv_heads)
    scale = 1.0 / math.sqrt(HD)
    row_id = grid_of((group_rows, 1), 0)
    row_slot = row_id % CAP
    row_head = row_id // (CAP * share)
    cache_load.wait()

    def near(i):
        base = pl.multiple_of(i * CAP, CAP)
        parts = [query_f[pl.ds(base, CAP), j * HD : (j + 1) * HD] for j in range(heads)]
        asked = jnp.concatenate(parts, 0).astype(jnp.bfloat16)
        rows = pl.ds(pl.multiple_of(i * group_rows, group_rows), group_rows)
        query_b[rows, :] = asked
        entries = cache[pl.ds(pl.multiple_of(i * span_rows, span_rows), span_rows), :]
        scores = lax.dot_general(
            asked, entries, (((1,), (1,)), ((), ())), preferred_element_type=jnp.float32
        )
        col = grid_of((1, span_rows), 1)
        width_l = 2 * kv_heads
        col_head = col % kv_heads
        col_code = (col // (width_l * live_span)) * kv_heads + col_head
        col_code = jnp.where((col % width_l) < kv_heads, col_code, -1)
        col_pos = (col // width_l) % live_span
        lengths = length_ref[...]
        which = grid_of((group_rows, lengths.shape[1]), 1) == i * CAP + row_slot
        limit = jnp.sum(jnp.where(which, lengths, 0), 1, keepdims=True)
        ok = (col_code == row_slot * kv_heads + row_head) & (col_pos < limit)
        scores = jnp.where(ok, scores * scale, -1e30)
        top = jnp.max(scores, 1, keepdims=True)
        weights = jnp.exp(scores - top)
        total = jnp.sum(weights, 1, keepdims=True)
        moved = pltpu.roll(weights, kv_heads, 1).astype(jnp.bfloat16)
        near_out[rows, :] = jnp.dot(moved, entries, preferred_element_type=jnp.float32)
        near_max[rows, :] = jnp.broadcast_to(top, (group_rows, HD))
        near_sum[rows, :] = jnp.broadcast_to(total, (group_rows, HD))

    def fresh(i):
        rows = slice(i * group_rows, (i + 1) * group_rows)
        each = group_rows // kv_heads
        found = []
        for h in range(kv_heads):
            asked = query_b[i * group_rows + h * each : i * group_rows + (h + 1) * each, :]
            found.append(
                lax.dot_general(
                    asked,
                    rbuf[1, i, :, h * HD : (h + 1) * HD],
                    (((1,), (1,)), ((), ())),
                    preferred_element_type=jnp.float32,
                )
            )
        scores = jnp.concatenate(found, 0)
        page = grid_of((1, every), 1) // owned_pages
        sent = (owner_row == me.astype(jnp.float32)) & (page == i)
        number = jnp.sum(jnp.where(sent, 1.0, 0.0), 1, keepdims=True)
        slot = grid_of((1, CAP * PAGE), 1) // PAGE
        ok = (slot == row_slot) & (slot.astype(jnp.float32) < number)
        scores = jnp.where(ok, scores * scale, -1e30)
        old_top = near_max[rows, :]
        top = jnp.maximum(jnp.max(scores, 1, keepdims=True), old_top)
        weights = jnp.where(ok, jnp.exp(scores - top), 0.0)
        keep = jnp.exp(old_top - top)
        total = near_sum[rows, :] * keep + jnp.sum(weights, 1, keepdims=True)
        weights = weights.astype(jnp.bfloat16)
        mixed = [
            jnp.dot(
                weights[h * each : (h + 1) * each, :],
                rbuf[0, i, :, h * HD : (h + 1) * HD],
                preferred_element_type=jnp.float32,
            )
            for h in range(kv_heads)
        ]
        final = (near_out[rows, :] * keep + jnp.concatenate(mixed, 0)) / total
        for j in range(heads):
            result[i * CAP : (i + 1) * CAP, j * HD : (j + 1) * HD] = final[
                j * CAP : (j + 1) * CAP, :
            ]

    half = count // 2

    def multiply(ph, index):
        span = pl.ds(pl.multiple_of(index * depth, depth), depth)

        @pl.loop(0, 2)
        def _(i):
            rows = pl.ds(pl.multiple_of(i * half, half), half)
            acc[ph, rows, :] += jnp.dot(
                tok[rows, span], wbuf[ph, index], preferred_element_type=jnp.float32
            )

    per_owner = slots // n_group

    def page_copy(ph, step):
        to = lax.rem(me + step, n_group)
        return send(
            obuf.at[ph, to], rbuf.at[ph, me], page_send.at[ph, to], page_recv.at[ph, me], to
        )

    def page_wait(ph, step):
        origin = lax.rem(me + step, n_group)
        send(
            obuf.at[ph, origin],
            rbuf.at[ph, origin],
            page_send.at[ph, origin],
            page_recv.at[ph, origin],
            origin,
        ).wait_recv()

    def hand_over(ph):
        held = acc[ph]
        if ph == 1:
            turned = [
                held[:, s : s + HD] * cos_ref[...]
                + pltpu.roll(held[:, s : s + HD], HD // 2, 1) * sin_ref[...]
                for s in range(0, cols, HD)
            ]
            held = jnp.concatenate(turned, -1)
        held = held.astype(jnp.bfloat16)

        for owner in range(n_group):
            rows = choose[owner * per_owner : (owner + 1) * per_owner, :]
            picked = jnp.dot(rows, held, preferred_element_type=jnp.float32)
            obuf[ph, owner] = picked.astype(jnp.bfloat16)
        for step in range(1, n_group):
            page_copy(ph, step).start()
        rbuf[ph, me] = obuf[ph, me]

    def at(step, way):
        ph = lax.div(step, line)
        dist = lax.rem(step, line)
        zz = z + dist * (2 * way - 1)
        live = (zz >= 0) & (zz < line) & ((dist > 0) | (way == 0))
        return ph, dist, zz, live

    def forward(ph, dist, zz, way, copy):
        @pl.when((way == 0) & (z < line - 1))
        def _():
            copy(ph, zz, True).start()

        @pl.when((way == 1) & (z > 0))
        def _():
            copy(ph, zz, False).start()

    @pl.loop(0, 2 * line + 1)
    def _(step):
        @pl.when(step < 2 * line)
        def _():
            @pl.loop(0, 2)
            def _(way):
                ph, dist, zz, live = at(step, way)

                @pl.when(live & (dist > 0))
                def _():
                    main_copy(ph, zz, True).wait_recv()
                    forward(ph, dist, zz, way, main_copy)
                    xhead_copy(ph, zz, x).start()

            @pl.loop(0, 2)
            def _(way):
                ph, dist, zz, live = at(step, way)

                @pl.when(live & (dist > 0))
                def _():
                    tail_copy(ph, zz, True).wait_recv()
                    forward(ph, dist, zz, way, tail_copy)

            @pl.when(step == 1)
            def _():
                start_own(1)

            @pl.when(step == 2)
            def _():
                pass_own_tail(1)

            @pl.loop(0, 2)
            def _(way):
                ph, dist, zz, live = at(step, way)

                @pl.when(live)
                def _():
                    multiply(ph, zz * 2 + x)

            near(step)

        @pl.when(step > 0)
        def _():
            @pl.loop(0, 2)
            def _(way):
                ph, dist, zz, live = at(step - 1, way)

                @pl.when(live)
                def _():
                    xhead_copy(ph, zz, peer_x).wait_recv()
                    multiply(ph, zz * 2 + peer_x)

        @pl.when(step == line)
        def _():
            hand_over(0)

    hand_over(1)
    for ph in range(2):
        for step in range(1, n_group):
            page_wait(ph, step)
    for i in range(n_group):
        fresh(i)
    out_ref[...] = result[...].astype(jnp.bfloat16)

    for ph in range(2):
        xtail_copy(ph, x).wait_send()
        for zz in range(line):
            xhead_copy(ph, zz, x).wait_send()

            @pl.when((z < line - 1) & (zz <= z))
            def _():
                main_copy(ph, zz, True).wait_send()
                tail_copy(ph, zz, True).wait_send()

            @pl.when((z > 0) & (zz >= z))
            def _():
                main_copy(ph, zz, False).wait_send()
                tail_copy(ph, zz, False).wait_send()

        for step in range(1, n_group):
            page_copy(ph, step).wait_send()


def per_device_fused(
    tokens, norm_gain, w_key, w_value, positions, page_owner, queries, kv_cache, cache_lengths
):
    count, width = tokens.shape
    depth, cols = w_key.shape
    n_group = lax.axis_size("group")
    line = n_group // 2
    slots = n_group * CAP * PAGE
    cut = depth - depth // 8
    rows = queries.shape[0]
    asked = rows * queries.shape[1] // HD
    cache = kv_cache.reshape(-1, HD)
    vmem = pl.BlockSpec(memory_space=pltpu.VMEM)
    hbm = pl.BlockSpec(memory_space=pl.ANY)
    dma = pltpu.SemaphoreType.DMA
    f32, bf16 = jnp.float32, jnp.bfloat16
    return pl.pallas_call(
        functools.partial(project_kernel, n_group, cut),
        out_shape=jax.ShapeDtypeStruct(queries.shape, bf16),
        in_specs=[hbm, vmem, hbm, hbm, vmem, vmem, vmem, hbm, vmem],
        out_specs=vmem,
        scratch_shapes=[
            pltpu.VMEM((count, width), bf16),
            pltpu.VMEM((2, n_group, depth, cols), bf16),
            pltpu.VMEM((2, count, cols), f32),
            pltpu.VMEM((slots, count), bf16),
            pltpu.VMEM((2, n_group, slots // n_group, cols), bf16),
            pltpu.VMEM((2, n_group, slots // n_group, cols), bf16),
            pltpu.VMEM((count, HD), f32),
            pltpu.VMEM((count, HD), f32),
            pltpu.VMEM(cache.shape, bf16),
            pltpu.VMEM(queries.shape, f32),
            pltpu.VMEM((asked, HD), bf16),
            pltpu.VMEM((asked, HD), f32),
            pltpu.VMEM((asked, HD), f32),
            pltpu.VMEM((asked, HD), f32),
            pltpu.VMEM(queries.shape, f32),
            dma,
            dma,
            dma((2,)),
            dma((2, line)),
            dma((2, line)),
            dma((2, line)),
            dma((2, line)),
            dma((2, line)),
            dma((2, line)),
            dma((2, line)),
            dma((2,)),
            dma((2, line)),
            dma((2, n_group)),
            dma((2, n_group)),
        ],
        compiler_params=pltpu.CompilerParams(
            collective_id=0, has_side_effects=True, vmem_limit_bytes=VMEM_BUDGET
        ),
        cost_estimate=pl.CostEstimate(
            flops=4 * count * width * cols,
            bytes_accessed=2 * count * width + 4 * depth * cols,
            transcendentals=0,
        ),
    )(
        tokens,
        norm_gain[None, :],
        w_key,
        w_value,
        positions[None, :],
        page_owner.reshape(1, -1),
        queries,
        cache,
        cache_lengths[None, :],
    )


def fits(count, width, cols, ngroup):
    slots = ngroup * CAP * PAGE
    held = 2 * count * width + 4 * width * cols + 8 * count * cols
    held += 2 * slots * count + 8 * slots * cols + 8 * count * HD
    return 3 * held < 2 * VMEM_BUDGET


def pick(tokens, norm_gain, w_key, *rest):
    ngroup = lax.axis_size("group")
    count, width = tokens.shape
    fused = ngroup % 2 == 0 and count % 256 == 0 and w_key.shape[0] % 1024 == 0
    fused = fused and fits(count, width, w_key.shape[1], ngroup)
    return (per_device_fused if fused else per_device)(tokens, norm_gain, w_key, *rest)


def solution(mesh):
    return jax.shard_map(
        pick,
        mesh=mesh,
        in_specs=(
            P("group", None),
            P(),
            P("group", "tensor"),
            P("group", "tensor"),
            P("group"),
            P(),
            P("group", "tensor"),
            P("group", None, None, "tensor", None),
            P("group"),
        ),
        out_specs=P("group", "tensor"),
        check_vma=False,
    )
```

```python
import functools
import math

import jax
import jax.numpy as jnp
from jax import lax
from jax.experimental import pallas as pl
from jax.experimental.pallas import tpu as pltpu
from jax.sharding import PartitionSpec as P

HD = 128
PAGE = 16
CAP = 8


def rotate(keys, positions):
    half = keys.shape[-1] // 2
    index = jnp.arange(half).astype(jnp.float32)
    inverse = jnp.exp(index * (-2.0 * math.log(500000.0) / keys.shape[-1]))
    angles = positions.astype(jnp.float32)[:, None] * inverse[None, :]
    cosine = jnp.cos(angles)[:, None, :]
    sine = jnp.sin(angles)[:, None, :]
    first = keys[..., :half]
    second = keys[..., half:]
    return jnp.concatenate([first * cosine - second * sine, second * cosine + first * sine], -1)


def attend(queries, kv_cache, placed, filled, lengths):
    count = queries.shape[0]
    heads = kv_cache.shape[3]
    span = kv_cache.shape[1]
    query_b = queries.reshape(count, heads, -1, HD)
    scale = 1.0 / math.sqrt(HD)
    near = (
        jnp.einsum(
            "rhgd,rlhd->rhgl", query_b, kv_cache[:, :, 0], preferred_element_type=jnp.float32
        )
        * scale
    )
    fresh = (
        jnp.einsum("rhgd,rphd->rhgp", query_b, placed[:, :, 0], preferred_element_type=jnp.float32)
        * scale
    )
    cache_ok = (jnp.arange(span)[None, :] < lengths[:, None])[:, None, None, :]
    page_ok = (filled > 0)[:, None, None, None]
    scores = jnp.concatenate(
        [jnp.where(cache_ok, near, -1e30), jnp.where(page_ok, fresh, -1e30)], -1
    )
    top = jnp.max(scores, -1, keepdims=True)
    weights = jnp.exp(scores - top)
    total = jnp.sum(weights, -1, keepdims=True)
    probs = (weights / total).astype(jnp.bfloat16)
    output = jnp.einsum(
        "rhgl,rlhd->rhgd", probs[..., :span], kv_cache[:, :, 1], preferred_element_type=jnp.float32
    )
    output = output + jnp.einsum(
        "rhgp,rphd->rhgd", probs[..., span:], placed[:, :, 1], preferred_element_type=jnp.float32
    )
    return output.reshape(count, -1).astype(jnp.bfloat16)


def per_device(
    tokens, norm_gain, w_key, w_value, positions, page_owner, queries, kv_cache, cache_lengths
):
    tok_count = tokens.shape[0]
    values = tokens.astype(jnp.float32)
    factor = lax.rsqrt(jnp.mean(values * values, -1, keepdims=True) + 1e-05)
    normed = (values * factor * norm_gain[None, :]).astype(jnp.bfloat16)
    full_key, full_value = (
        lax.all_gather(w_key, "group", axis=0, tiled=True),
        lax.all_gather(w_value, "group", axis=0, tiled=True),
    )
    key_sum = jnp.dot(normed, full_key, preferred_element_type=jnp.float32)
    value_sum = jnp.dot(normed, full_value, preferred_element_type=jnp.float32)
    heads = w_key.shape[1] // HD
    keys = rotate(key_sum.reshape(tok_count, heads, HD), positions).astype(jnp.bfloat16)
    vals = value_sum.astype(jnp.bfloat16).reshape(tok_count, heads, HD)
    pages = tok_count // PAGE
    page_kv = jnp.stack([keys, vals], 1).reshape(pages, PAGE * 2 * heads * HD)
    ngroup = lax.axis_size("group")
    myself = lax.axis_index("group")
    owners_all = page_owner[:, 0].reshape(ngroup, pages)
    owned = lax.dynamic_index_in_dim(owners_all, myself, 0, keepdims=False)
    onehot = (owned[:, None] == jnp.arange(ngroup)[None, :]).astype(jnp.float32)
    earlier = (jnp.arange(pages)[:, None] > jnp.arange(pages)[None, :]).astype(jnp.float32)
    before = jnp.dot(earlier, onehot, preferred_element_type=jnp.float32)
    rank = jnp.sum(before * onehot, 1).astype(jnp.int32)
    target = owned * CAP + rank
    chooser = (jnp.arange(ngroup * CAP)[:, None] == target[None, :]).astype(jnp.bfloat16)
    outgoing = jnp.dot(chooser, page_kv, preferred_element_type=jnp.float32).astype(jnp.bfloat16)
    outgoing = outgoing.reshape(ngroup * CAP, PAGE, 2, heads, HD)
    received = lax.all_to_all(outgoing, "group", split_axis=0, concat_axis=0, tiled=True)
    counts = jnp.sum((owners_all == myself).astype(jnp.int32), 1)
    filled = (jnp.arange(CAP)[None, :] < counts[:, None]).reshape(-1).astype(jnp.int32)
    return attend(queries, kv_cache, received, filled, cache_lengths)


MESH = pl.DeviceIdType.MESH
VMEM_BUDGET = 56 * 2**20
TAIL_LAG = 2
PEER_LAG = 5


def project_kernel(
    n_group,
    cut,
    tok_ref,
    gain_ref,
    wk_ref,
    wv_ref,
    pos_ref,
    owner_ref,
    query_ref,
    cache_ref,
    length_ref,
    out_ref,
    tok,
    wbuf,
    acc,
    choose,
    obuf,
    rbuf,
    cos_ref,
    sin_ref,
    cache,
    query_f,
    query_b,
    near_out,
    near_max,
    near_sum,
    result,
    tok_sem,
    cache_sem,
    own_sem,
    up_sem,
    down_sem,
    main_sem,
    tail_up_sem,
    tail_down_sem,
    tail_sem,
    xhead_send,
    xtail_send,
    xhead_sem,
    page_send,
    page_recv,
):
    line = n_group // 2
    depth, cols = wk_ref.shape
    count = tok.shape[0]
    me = lax.axis_index("group")
    mine = lax.axis_index("tensor")
    z = lax.div(me, 2)
    x = lax.rem(me, 2)
    peer_x = 1 - x
    peer = z * 2 + peer_x
    head_rows = pl.ds(0, cut)
    tail_rows = pl.ds(cut, depth - cut)

    def send(src, dst, send_sem, recv_sem, group):
        return pltpu.make_async_remote_copy(
            src_ref=src,
            dst_ref=dst,
            send_sem=send_sem,
            recv_sem=recv_sem,
            device_id=(group, mine),
            device_id_type=MESH,
        )

    def block(ph, zz, xx):
        return wbuf.at[ph, zz * 2 + xx]

    def main_copy(ph, zz, up, src=None):
        src = block(ph, zz, x) if src is None else src
        sem, to = (up_sem, me + 2) if up else (down_sem, me - 2)
        return send(src, block(ph, zz, x), sem.at[ph, zz], main_sem.at[ph, zz], to)

    def tail_copy(ph, zz, up):
        part = wbuf.at[ph, zz * 2 + peer_x, tail_rows]
        sem, to = (tail_up_sem, me + 2) if up else (tail_down_sem, me - 2)
        return send(part, part, sem.at[ph, zz], tail_sem.at[ph, zz], to)

    def xhead_copy(ph, zz, column):
        part = wbuf.at[ph, zz * 2 + column, head_rows]
        return send(part, part, xhead_send.at[ph, zz], xhead_sem.at[ph, zz], peer)

    def xtail_copy(ph, column):
        part = wbuf.at[ph, z * 2 + column, tail_rows]
        return send(part, part, xtail_send.at[ph], tail_sem.at[ph, z], peer)

    def both_ways(make):
        @pl.when(z < line - 1)
        def _():
            make(True)

        @pl.when(z > 0)
        def _():
            make(False)

    kv_heads = cols // HD
    phases = 2 * kv_heads

    def own_load(ph):
        ref, h = (wv_ref, ph) if ph < kv_heads else (wk_ref, ph - kv_heads)
        return pltpu.make_async_copy(
            ref.at[:, h * HD : (h + 1) * HD], wbuf.at[ph, me], own_sem.at[ph]
        )

    def start_own(ph):
        both_ways(lambda up: main_copy(ph, z, up).start())
        xtail_copy(ph, x).start()
        xhead_copy(ph, z, x).start()

    def pass_own_tail(ph):
        xtail_copy(ph, peer_x).wait_recv()
        both_ways(lambda up: tail_copy(ph, z, up).start())

    for ph in range(phases):
        own_load(ph).start()
    tok_load = pltpu.make_async_copy(tok_ref, tok, tok_sem)
    tok_load.start()
    cache_load = pltpu.make_async_copy(cache_ref, cache, cache_sem)
    cache_load.start()

    barrier = pltpu.get_barrier_semaphore()
    for step in range(1, n_group):
        pl.semaphore_signal(
            barrier,
            inc=1,
            device_id=(lax.rem(me + step, n_group), mine),
            device_id_type=MESH,
        )
    pl.semaphore_wait(barrier, n_group - 1)

    for ph in range(phases):
        own_load(ph).wait()
        if ph < 2:
            start_own(ph)
    acc[...] = jnp.zeros_like(acc)
    tok_load.wait()

    chunk = 32
    width = tok.shape[1]
    piece = 1024

    @pl.loop(0, count // chunk)
    def _(i):
        rows = pl.ds(pl.multiple_of(i * chunk, chunk), chunk)
        total = jnp.zeros((chunk, 128), jnp.float32)
        for k in range(width // piece):
            part = tok[rows, k * piece : (k + 1) * piece].astype(jnp.float32)
            part = part * part
            for j in range(piece // 128):
                total = total + part[:, j * 128 : (j + 1) * 128]
        mean = jnp.sum(total, -1, keepdims=True) * (1.0 / width)
        factor = lax.rsqrt(mean + 1e-05)
        for k in range(width // piece):
            span = slice(k * piece, (k + 1) * piece)
            part = tok[rows, span].astype(jnp.float32) * factor * gain_ref[:, span]
            tok[rows, span] = part.astype(jnp.bfloat16)

    pass_own_tail(0)

    slots = choose.shape[0]
    owned_pages = count // PAGE
    every = owner_ref.shape[1]

    def grid_of(shape, dim):
        return lax.broadcasted_iota(jnp.int32, shape, dim)

    def column(row):
        size = row.shape[1]
        same = grid_of((size, size), 0) == grid_of((size, size), 1)
        return jnp.sum(jnp.where(same, row, 0), 1, keepdims=True)

    owner_row = owner_ref[...].astype(jnp.float32)
    owner_col = column(owner_row)
    first = grid_of((every, every), 0)
    second = grid_of((every, every), 1)
    before = (owner_col == owner_row) & (first < second)
    before = before & (first // owned_pages == second // owned_pages)
    rank = jnp.sum(jnp.where(before, 1.0, 0.0), 0, keepdims=True)
    place = owner_row * CAP + rank
    page_of = grid_of((every, count), 0) == me * owned_pages + grid_of((every, count), 1) // PAGE
    place_col = column(place)
    token_place = jnp.sum(jnp.where(page_of, place_col, 0.0), 0, keepdims=True)
    token_row = token_place.astype(jnp.int32) * PAGE + grid_of((1, count), 1) % PAGE

    lane = grid_of((1, HD), 1)
    index = (lane % (HD // 2)).astype(jnp.float32)
    inverse = jnp.exp(index * (-2.0 * math.log(500000.0) / HD))
    for start in range(0, count, 128):
        angles = column(pos_ref[:, start : start + 128].astype(jnp.float32)) * inverse
        cos_ref[start : start + 128, :] = jnp.cos(angles)
        turn = jnp.sin(angles)
        sin_ref[start : start + 128, :] = jnp.where(lane < HD // 2, -turn, turn)

    @pl.loop(0, slots // 128)
    def _(i):
        start = pl.multiple_of(i * 128, 128)
        row = lax.broadcasted_iota(jnp.int32, (128, count), 0) + start
        hit = row == token_row
        choose[pl.ds(start, 128), :] = jnp.where(hit, 1.0, 0.0).astype(jnp.bfloat16)

    query_f[...] = query_ref[...].astype(jnp.float32)
    heads = query_f.shape[1] // HD
    share = heads // kv_heads
    group_rows = heads * CAP
    span_rows = cache.shape[0] // n_group
    live_span = span_rows // (CAP * 2 * kv_heads)
    scale = 1.0 / math.sqrt(HD)
    row_id = grid_of((group_rows, 1), 0)
    row_slot = row_id % CAP
    row_head = row_id // (CAP * share)
    cache_load.wait()

    def near(i):
        base = pl.multiple_of(i * CAP, CAP)
        parts = [query_f[pl.ds(base, CAP), j * HD : (j + 1) * HD] for j in range(heads)]
        asked = jnp.concatenate(parts, 0).astype(jnp.bfloat16)
        rows = pl.ds(pl.multiple_of(i * group_rows, group_rows), group_rows)
        query_b[rows, :] = asked
        entries = cache[pl.ds(pl.multiple_of(i * span_rows, span_rows), span_rows), :]
        scores = lax.dot_general(
            asked, entries, (((1,), (1,)), ((), ())), preferred_element_type=jnp.float32
        )
        col = grid_of((1, span_rows), 1)
        width_l = 2 * kv_heads
        col_head = col % kv_heads
        col_code = (col // (width_l * live_span)) * kv_heads + col_head
        col_code = jnp.where((col % width_l) < kv_heads, col_code, -1)
        col_pos = (col // width_l) % live_span
        lengths = length_ref[...]
        which = grid_of((group_rows, lengths.shape[1]), 1) == i * CAP + row_slot
        limit = jnp.sum(jnp.where(which, lengths, 0), 1, keepdims=True)
        ok = (col_code == row_slot * kv_heads + row_head) & (col_pos < limit)
        scores = jnp.where(ok, scores * scale, -1e30)
        top = jnp.max(scores, 1, keepdims=True)
        weights = jnp.exp(scores - top)
        total = jnp.sum(weights, 1, keepdims=True)
        moved = pltpu.roll(weights, kv_heads, 1).astype(jnp.bfloat16)
        near_out[rows, :] = jnp.dot(moved, entries, preferred_element_type=jnp.float32)
        near_max[rows, :] = jnp.broadcast_to(top, (group_rows, HD))
        near_sum[rows, :] = jnp.broadcast_to(total, (group_rows, HD))

    each = group_rows // kv_heads

    def fresh(i, h):
        rows = slice(i * group_rows + h * each, i * group_rows + (h + 1) * each)
        scores = lax.dot_general(
            query_b[rows, :],
            rbuf[kv_heads + h, i],
            (((1,), (1,)), ((), ())),
            preferred_element_type=jnp.float32,
        )
        page = grid_of((1, every), 1) // owned_pages
        sent = (owner_row == me.astype(jnp.float32)) & (page == i)
        number = jnp.sum(jnp.where(sent, 1.0, 0.0), 1, keepdims=True)
        slot = grid_of((1, CAP * PAGE), 1) // PAGE
        ok = (slot == grid_of((each, 1), 0) % CAP) & (slot.astype(jnp.float32) < number)
        scores = jnp.where(ok, scores * scale, -1e30)
        old_top = near_max[rows, :]
        top = jnp.maximum(jnp.max(scores, 1, keepdims=True), old_top)
        weights = jnp.where(ok, jnp.exp(scores - top), 0.0)
        keep = jnp.exp(old_top - top)
        total = near_sum[rows, :] * keep + jnp.sum(weights, 1, keepdims=True)
        mixed = jnp.dot(
            weights.astype(jnp.bfloat16), rbuf[h, i], preferred_element_type=jnp.float32
        )
        final = (near_out[rows, :] * keep + mixed) / total
        for j in range(share):
            at_col = (h * share + j) * HD
            result[i * CAP : (i + 1) * CAP, at_col : at_col + HD] = final[
                j * CAP : (j + 1) * CAP, :
            ]

    def finish(h):
        for ph in (h, kv_heads + h):
            for step in range(1, n_group):
                page_wait(ph, step)
        for i in range(n_group):
            fresh(i, h)
        span = slice(h * share * HD, (h + 1) * share * HD)
        out_ref[:, span] = result[:, span].astype(jnp.bfloat16)

    half = count // 2

    def multiply(ph, index):
        span = pl.ds(pl.multiple_of(index * depth, depth), depth)

        @pl.loop(0, 2)
        def _(i):
            rows = pl.ds(pl.multiple_of(i * half, half), half)
            acc[ph, rows, :] += jnp.dot(
                tok[rows, span], wbuf[ph, index], preferred_element_type=jnp.float32
            )

    per_owner = slots // n_group

    def page_copy(ph, step):
        to = lax.rem(me + step, n_group)
        return send(
            obuf.at[ph, to], rbuf.at[ph, me], page_send.at[ph, to], page_recv.at[ph, me], to
        )

    def page_wait(ph, step):
        origin = lax.rem(me + step, n_group)
        send(
            obuf.at[ph, origin],
            rbuf.at[ph, origin],
            page_send.at[ph, origin],
            page_recv.at[ph, origin],
            origin,
        ).wait_recv()

    def hand_over(ph):
        held = acc[ph]
        if ph >= kv_heads:
            held = held * cos_ref[...] + pltpu.roll(held, HD // 2, 1) * sin_ref[...]
        held = held.astype(jnp.bfloat16)

        for owner in range(n_group):
            rows = choose[owner * per_owner : (owner + 1) * per_owner, :]
            picked = jnp.dot(rows, held, preferred_element_type=jnp.float32)
            obuf[ph, owner] = picked.astype(jnp.bfloat16)
        for step in range(1, n_group):
            page_copy(ph, step).start()
        rbuf[ph, me] = obuf[ph, me]

    def at(step, way):
        ph = lax.div(step, line)
        dist = lax.rem(step, line)
        zz = z + dist * (2 * way - 1)
        live = (zz >= 0) & (zz < line) & ((dist > 0) | (way == 0))
        return ph, dist, zz, live

    def forward(ph, dist, zz, way, copy):
        @pl.when((way == 0) & (z < line - 1))
        def _():
            copy(ph, zz, True).start()

        @pl.when((way == 1) & (z > 0))
        def _():
            copy(ph, zz, False).start()

    @pl.loop(0, phases * line + PEER_LAG)
    def _(step):
        @pl.when(step < phases * line)
        def _():
            @pl.loop(0, 2)
            def _(way):
                ph, dist, zz, live = at(step, way)

                @pl.when(live & (dist > 0))
                def _():
                    main_copy(ph, zz, True).wait_recv()
                    forward(ph, dist, zz, way, main_copy)
                    xhead_copy(ph, zz, x).start()

            following = lax.div(step, line) + 1

            @pl.when((lax.rem(step, line) == 1) & (following + 1 < phases))
            def _():
                start_own(following + 1)

            @pl.when((lax.rem(step, line) == 2) & (following < phases))
            def _():
                pass_own_tail(following)

            @pl.loop(0, 2)
            def _(way):
                ph, dist, zz, live = at(step, way)

                @pl.when(live)
                def _():
                    multiply(ph, zz * 2 + x)

            @pl.when(step < n_group)
            def _():
                near(step)

        @pl.when((step >= TAIL_LAG) & (step < phases * line + TAIL_LAG))
        def _():
            @pl.loop(0, 2)
            def _(way):
                ph, dist, zz, live = at(step - TAIL_LAG, way)

                @pl.when(live & (dist > 0))
                def _():
                    tail_copy(ph, zz, True).wait_recv()
                    forward(ph, dist, zz, way, tail_copy)

        @pl.when(step >= PEER_LAG)
        def _():
            @pl.loop(0, 2)
            def _(way):
                ph, dist, zz, live = at(step - PEER_LAG, way)

                @pl.when(live)
                def _():
                    xhead_copy(ph, zz, peer_x).wait_recv()
                    multiply(ph, zz * 2 + peer_x)

        for ph in range(phases - 1):

            @pl.when(step == (ph + 1) * line + PEER_LAG - 1)
            def _():
                hand_over(ph)

    hand_over(phases - 1)
    for h in range(kv_heads):
        finish(h)

    for ph in range(phases):
        xtail_copy(ph, x).wait_send()
        for zz in range(line):
            xhead_copy(ph, zz, x).wait_send()

            @pl.when((z < line - 1) & (zz <= z))
            def _():
                main_copy(ph, zz, True).wait_send()
                tail_copy(ph, zz, True).wait_send()

            @pl.when((z > 0) & (zz >= z))
            def _():
                main_copy(ph, zz, False).wait_send()
                tail_copy(ph, zz, False).wait_send()

        for step in range(1, n_group):
            page_copy(ph, step).wait_send()


def per_device_fused(
    tokens, norm_gain, w_key, w_value, positions, page_owner, queries, kv_cache, cache_lengths
):
    count, width = tokens.shape
    depth, cols = w_key.shape
    n_group = lax.axis_size("group")
    line = n_group // 2
    slots = n_group * CAP * PAGE
    cut = depth - depth // 8
    phases = 2 * cols // HD
    rows = queries.shape[0]
    asked = rows * queries.shape[1] // HD
    cache = kv_cache.reshape(-1, HD)
    vmem = pl.BlockSpec(memory_space=pltpu.VMEM)
    hbm = pl.BlockSpec(memory_space=pl.ANY)
    dma = pltpu.SemaphoreType.DMA
    f32, bf16 = jnp.float32, jnp.bfloat16
    return pl.pallas_call(
        functools.partial(project_kernel, n_group, cut),
        out_shape=jax.ShapeDtypeStruct(queries.shape, bf16),
        in_specs=[hbm, vmem, hbm, hbm, vmem, vmem, vmem, hbm, vmem],
        out_specs=vmem,
        scratch_shapes=[
            pltpu.VMEM((count, width), bf16),
            pltpu.VMEM((phases, n_group, depth, HD), bf16),
            pltpu.VMEM((phases, count, HD), f32),
            pltpu.VMEM((slots, count), bf16),
            pltpu.VMEM((phases, n_group, slots // n_group, HD), bf16),
            pltpu.VMEM((phases, n_group, slots // n_group, HD), bf16),
            pltpu.VMEM((count, HD), f32),
            pltpu.VMEM((count, HD), f32),
            pltpu.VMEM(cache.shape, bf16),
            pltpu.VMEM(queries.shape, f32),
            pltpu.VMEM((asked, HD), bf16),
            pltpu.VMEM((asked, HD), f32),
            pltpu.VMEM((asked, HD), f32),
            pltpu.VMEM((asked, HD), f32),
            pltpu.VMEM(queries.shape, f32),
            dma,
            dma,
            dma((phases,)),
            dma((phases, line)),
            dma((phases, line)),
            dma((phases, line)),
            dma((phases, line)),
            dma((phases, line)),
            dma((phases, line)),
            dma((phases, line)),
            dma((phases,)),
            dma((phases, line)),
            dma((phases, n_group)),
            dma((phases, n_group)),
        ],
        compiler_params=pltpu.CompilerParams(
            collective_id=0, has_side_effects=True, vmem_limit_bytes=VMEM_BUDGET
        ),
        cost_estimate=pl.CostEstimate(
            flops=4 * count * width * cols,
            bytes_accessed=2 * count * width + 4 * depth * cols,
            transcendentals=0,
        ),
    )(
        tokens,
        norm_gain[None, :],
        w_key,
        w_value,
        positions[None, :],
        page_owner.reshape(1, -1),
        queries,
        cache,
        cache_lengths[None, :],
    )


def fits(count, width, cols, ngroup):
    slots = ngroup * CAP * PAGE
    held = 2 * count * width + 4 * width * cols + 8 * count * cols
    held += 2 * slots * count + 8 * slots * cols + 8 * count * HD
    return 3 * held < 2 * VMEM_BUDGET


def pick(tokens, norm_gain, w_key, *rest):
    ngroup = lax.axis_size("group")
    count, width = tokens.shape
    fused = ngroup >= 6 and ngroup % 2 == 0 and count % 256 == 0 and w_key.shape[0] % 1024 == 0
    fused = fused and fits(count, width, w_key.shape[1], ngroup)
    return (per_device_fused if fused else per_device)(tokens, norm_gain, w_key, *rest)


def solution(mesh):
    return jax.shard_map(
        pick,
        mesh=mesh,
        in_specs=(
            P("group", None),
            P(),
            P("group", "tensor"),
            P("group", "tensor"),
            P("group"),
            P(),
            P("group", "tensor"),
            P("group", None, None, "tensor", None),
            P("group"),
        ),
        out_specs=P("group", "tensor"),
        check_vma=False,
    )
```

```python
import functools
import math

import jax
import jax.numpy as jnp
from jax import lax
from jax.experimental import pallas as pl
from jax.experimental.pallas import tpu as pltpu
from jax.sharding import PartitionSpec as P

HD = 128
PAGE = 16
CAP = 8


def rotate(keys, positions):
    half = keys.shape[-1] // 2
    index = jnp.arange(half).astype(jnp.float32)
    inverse = jnp.exp(index * (-2.0 * math.log(500000.0) / keys.shape[-1]))
    angles = positions.astype(jnp.float32)[:, None] * inverse[None, :]
    cosine = jnp.cos(angles)[:, None, :]
    sine = jnp.sin(angles)[:, None, :]
    first = keys[..., :half]
    second = keys[..., half:]
    return jnp.concatenate([first * cosine - second * sine, second * cosine + first * sine], -1)


def attend(queries, kv_cache, placed, filled, lengths):
    count = queries.shape[0]
    heads = kv_cache.shape[3]
    span = kv_cache.shape[1]
    query_b = queries.reshape(count, heads, -1, HD)
    scale = 1.0 / math.sqrt(HD)
    near = (
        jnp.einsum(
            "rhgd,rlhd->rhgl", query_b, kv_cache[:, :, 0], preferred_element_type=jnp.float32
        )
        * scale
    )
    fresh = (
        jnp.einsum("rhgd,rphd->rhgp", query_b, placed[:, :, 0], preferred_element_type=jnp.float32)
        * scale
    )
    cache_ok = (jnp.arange(span)[None, :] < lengths[:, None])[:, None, None, :]
    page_ok = (filled > 0)[:, None, None, None]
    scores = jnp.concatenate(
        [jnp.where(cache_ok, near, -1e30), jnp.where(page_ok, fresh, -1e30)], -1
    )
    top = jnp.max(scores, -1, keepdims=True)
    weights = jnp.exp(scores - top)
    total = jnp.sum(weights, -1, keepdims=True)
    probs = (weights / total).astype(jnp.bfloat16)
    output = jnp.einsum(
        "rhgl,rlhd->rhgd", probs[..., :span], kv_cache[:, :, 1], preferred_element_type=jnp.float32
    )
    output = output + jnp.einsum(
        "rhgp,rphd->rhgd", probs[..., span:], placed[:, :, 1], preferred_element_type=jnp.float32
    )
    return output.reshape(count, -1).astype(jnp.bfloat16)


def per_device(
    tokens, norm_gain, w_key, w_value, positions, page_owner, queries, kv_cache, cache_lengths
):
    tok_count = tokens.shape[0]
    values = tokens.astype(jnp.float32)
    factor = lax.rsqrt(jnp.mean(values * values, -1, keepdims=True) + 1e-05)
    normed = (values * factor * norm_gain[None, :]).astype(jnp.bfloat16)
    full_key, full_value = (
        lax.all_gather(w_key, "group", axis=0, tiled=True),
        lax.all_gather(w_value, "group", axis=0, tiled=True),
    )
    key_sum = jnp.dot(normed, full_key, preferred_element_type=jnp.float32)
    value_sum = jnp.dot(normed, full_value, preferred_element_type=jnp.float32)
    heads = w_key.shape[1] // HD
    keys = rotate(key_sum.reshape(tok_count, heads, HD), positions).astype(jnp.bfloat16)
    vals = value_sum.astype(jnp.bfloat16).reshape(tok_count, heads, HD)
    pages = tok_count // PAGE
    page_kv = jnp.stack([keys, vals], 1).reshape(pages, PAGE * 2 * heads * HD)
    ngroup = lax.axis_size("group")
    myself = lax.axis_index("group")
    owners_all = page_owner[:, 0].reshape(ngroup, pages)
    owned = lax.dynamic_index_in_dim(owners_all, myself, 0, keepdims=False)
    onehot = (owned[:, None] == jnp.arange(ngroup)[None, :]).astype(jnp.float32)
    earlier = (jnp.arange(pages)[:, None] > jnp.arange(pages)[None, :]).astype(jnp.float32)
    before = jnp.dot(earlier, onehot, preferred_element_type=jnp.float32)
    rank = jnp.sum(before * onehot, 1).astype(jnp.int32)
    target = owned * CAP + rank
    chooser = (jnp.arange(ngroup * CAP)[:, None] == target[None, :]).astype(jnp.bfloat16)
    outgoing = jnp.dot(chooser, page_kv, preferred_element_type=jnp.float32).astype(jnp.bfloat16)
    outgoing = outgoing.reshape(ngroup * CAP, PAGE, 2, heads, HD)
    received = lax.all_to_all(outgoing, "group", split_axis=0, concat_axis=0, tiled=True)
    counts = jnp.sum((owners_all == myself).astype(jnp.int32), 1)
    filled = (jnp.arange(CAP)[None, :] < counts[:, None]).reshape(-1).astype(jnp.int32)
    return attend(queries, kv_cache, received, filled, cache_lengths)


MESH = pl.DeviceIdType.MESH
VMEM_BUDGET = 56 * 2**20
TAIL_LAG = 2
PEER_LAG = 5


def project_kernel(
    n_group,
    cut,
    tok_ref,
    gain_ref,
    wk_ref,
    wv_ref,
    pos_ref,
    owner_ref,
    query_ref,
    cache_ref,
    length_ref,
    out_ref,
    tok,
    wbuf,
    acc,
    choose,
    obuf,
    rbuf,
    cos_ref,
    sin_ref,
    cache,
    query_f,
    query_b,
    near_out,
    near_max,
    near_sum,
    result,
    tok_sem,
    cache_sem,
    own_sem,
    up_sem,
    down_sem,
    main_sem,
    tail_up_sem,
    tail_down_sem,
    tail_sem,
    xhead_send,
    xtail_send,
    xhead_sem,
    page_send,
    page_recv,
):
    line = n_group // 2
    depth, cols = wk_ref.shape
    count = tok.shape[0]
    me = lax.axis_index("group")
    mine = lax.axis_index("tensor")
    z = lax.div(me, 2)
    x = lax.rem(me, 2)
    peer_x = 1 - x
    peer = z * 2 + peer_x
    head_rows = pl.ds(0, cut)
    tail_rows = pl.ds(cut, depth - cut)

    def send(src, dst, send_sem, recv_sem, group):
        return pltpu.make_async_remote_copy(
            src_ref=src,
            dst_ref=dst,
            send_sem=send_sem,
            recv_sem=recv_sem,
            device_id=(group, mine),
            device_id_type=MESH,
        )

    def block(ph, zz, xx):
        return wbuf.at[ph, zz * 2 + xx]

    def main_copy(ph, zz, up, src=None):
        src = block(ph, zz, x) if src is None else src
        sem, to = (up_sem, me + 2) if up else (down_sem, me - 2)
        return send(src, block(ph, zz, x), sem.at[ph, zz], main_sem.at[ph, zz], to)

    def tail_copy(ph, zz, up):
        part = wbuf.at[ph, zz * 2 + peer_x, tail_rows]
        sem, to = (tail_up_sem, me + 2) if up else (tail_down_sem, me - 2)
        return send(part, part, sem.at[ph, zz], tail_sem.at[ph, zz], to)

    def xhead_copy(ph, zz, column):
        part = wbuf.at[ph, zz * 2 + column, head_rows]
        return send(part, part, xhead_send.at[ph, zz], xhead_sem.at[ph, zz], peer)

    def xtail_copy(ph, column):
        part = wbuf.at[ph, z * 2 + column, tail_rows]
        return send(part, part, xtail_send.at[ph], tail_sem.at[ph, z], peer)

    def both_ways(make):
        @pl.when(z < line - 1)
        def _():
            make(True)

        @pl.when(z > 0)
        def _():
            make(False)

    kv_heads = cols // HD
    phases = 2 * kv_heads

    def own_load(ph):
        ref, h = (wv_ref, ph) if ph < kv_heads else (wk_ref, ph - kv_heads)
        return pltpu.make_async_copy(
            ref.at[:, h * HD : (h + 1) * HD], wbuf.at[ph, me], own_sem.at[ph]
        )

    def start_own(ph):
        both_ways(lambda up: main_copy(ph, z, up).start())
        xtail_copy(ph, x).start()
        xhead_copy(ph, z, x).start()

    def pass_own_tail(ph):
        xtail_copy(ph, peer_x).wait_recv()
        both_ways(lambda up: tail_copy(ph, z, up).start())

    for ph in range(phases):
        own_load(ph).start()
    tok_load = pltpu.make_async_copy(tok_ref, tok, tok_sem)
    tok_load.start()
    cache_load = pltpu.make_async_copy(cache_ref, cache, cache_sem)
    cache_load.start()

    barrier = pltpu.get_barrier_semaphore()
    for step in range(1, n_group):
        pl.semaphore_signal(
            barrier,
            inc=1,
            device_id=(lax.rem(me + step, n_group), mine),
            device_id_type=MESH,
        )
    pl.semaphore_wait(barrier, n_group - 1)

    for ph in range(phases):
        own_load(ph).wait()
        if ph < 2:
            start_own(ph)
    acc[...] = jnp.zeros_like(acc)
    tok_load.wait()

    chunk = 32
    width = tok.shape[1]
    piece = 1024

    @pl.loop(0, count // chunk)
    def _(i):
        rows = pl.ds(pl.multiple_of(i * chunk, chunk), chunk)
        total = jnp.zeros((chunk, 128), jnp.float32)
        for k in range(width // piece):
            part = tok[rows, k * piece : (k + 1) * piece].astype(jnp.float32)
            part = part * part
            for j in range(piece // 128):
                total = total + part[:, j * 128 : (j + 1) * 128]
        mean = jnp.sum(total, -1, keepdims=True) * (1.0 / width)
        factor = lax.rsqrt(mean + 1e-05)
        for k in range(width // piece):
            span = slice(k * piece, (k + 1) * piece)
            part = tok[rows, span].astype(jnp.float32) * factor * gain_ref[:, span]
            tok[rows, span] = part.astype(jnp.bfloat16)

    pass_own_tail(0)

    slots = choose.shape[0]
    owned_pages = count // PAGE
    every = owner_ref.shape[1]

    def grid_of(shape, dim):
        return lax.broadcasted_iota(jnp.int32, shape, dim)

    def column(row):
        size = row.shape[1]
        same = grid_of((size, size), 0) == grid_of((size, size), 1)
        return jnp.sum(jnp.where(same, row, 0), 1, keepdims=True)

    owner_row = owner_ref[...].astype(jnp.float32)
    owner_col = column(owner_row)
    first = grid_of((every, every), 0)
    second = grid_of((every, every), 1)
    before = (owner_col == owner_row) & (first < second)
    before = before & (first // owned_pages == second // owned_pages)
    rank = jnp.sum(jnp.where(before, 1.0, 0.0), 0, keepdims=True)
    place = owner_row * CAP + rank
    page_of = grid_of((every, count), 0) == me * owned_pages + grid_of((every, count), 1) // PAGE
    place_col = column(place)
    token_place = jnp.sum(jnp.where(page_of, place_col, 0.0), 0, keepdims=True)
    token_row = token_place.astype(jnp.int32) * PAGE + grid_of((1, count), 1) % PAGE

    lane = grid_of((1, HD), 1)
    index = (lane % (HD // 2)).astype(jnp.float32)
    inverse = jnp.exp(index * (-2.0 * math.log(500000.0) / HD))
    for start in range(0, count, 128):
        angles = column(pos_ref[:, start : start + 128].astype(jnp.float32)) * inverse
        cos_ref[start : start + 128, :] = jnp.cos(angles)
        turn = jnp.sin(angles)
        sin_ref[start : start + 128, :] = jnp.where(lane < HD // 2, -turn, turn)

    @pl.loop(0, slots // 128)
    def _(i):
        start = pl.multiple_of(i * 128, 128)
        row = lax.broadcasted_iota(jnp.int32, (128, count), 0) + start
        hit = row == token_row
        choose[pl.ds(start, 128), :] = jnp.where(hit, 1.0, 0.0).astype(jnp.bfloat16)

    query_f[...] = query_ref[...].astype(jnp.float32)
    heads = query_f.shape[1] // HD
    share = heads // kv_heads
    group_rows = heads * CAP
    span_rows = cache.shape[0] // n_group
    live_span = span_rows // (CAP * 2 * kv_heads)
    scale = 1.0 / math.sqrt(HD)
    row_id = grid_of((group_rows, 1), 0)
    row_slot = row_id % CAP
    row_head = row_id // (CAP * share)
    cache_load.wait()

    def near(i):
        base = pl.multiple_of(i * CAP, CAP)
        parts = [query_f[pl.ds(base, CAP), j * HD : (j + 1) * HD] for j in range(heads)]
        asked = jnp.concatenate(parts, 0).astype(jnp.bfloat16)
        rows = pl.ds(pl.multiple_of(i * group_rows, group_rows), group_rows)
        query_b[rows, :] = asked
        entries = cache[pl.ds(pl.multiple_of(i * span_rows, span_rows), span_rows), :]
        scores = lax.dot_general(
            asked, entries, (((1,), (1,)), ((), ())), preferred_element_type=jnp.float32
        )
        col = grid_of((1, span_rows), 1)
        width_l = 2 * kv_heads
        col_head = col % kv_heads
        col_code = (col // (width_l * live_span)) * kv_heads + col_head
        col_code = jnp.where((col % width_l) < kv_heads, col_code, -1)
        col_pos = (col // width_l) % live_span
        lengths = length_ref[...]
        which = grid_of((group_rows, lengths.shape[1]), 1) == i * CAP + row_slot
        limit = jnp.sum(jnp.where(which, lengths, 0), 1, keepdims=True)
        ok = (col_code == row_slot * kv_heads + row_head) & (col_pos < limit)
        scores = jnp.where(ok, scores * scale, -1e30)
        top = jnp.max(scores, 1, keepdims=True)
        weights = jnp.exp(scores - top)
        total = jnp.sum(weights, 1, keepdims=True)
        moved = pltpu.roll(weights, kv_heads, 1).astype(jnp.bfloat16)
        near_out[rows, :] = jnp.dot(moved, entries, preferred_element_type=jnp.float32)
        near_max[rows, :] = jnp.broadcast_to(top, (group_rows, HD))
        near_sum[rows, :] = jnp.broadcast_to(total, (group_rows, HD))

    each = group_rows // kv_heads

    def fresh(i, h):
        rows = slice(i * group_rows + h * each, i * group_rows + (h + 1) * each)
        scores = lax.dot_general(
            query_b[rows, :],
            rbuf[kv_heads + h, i],
            (((1,), (1,)), ((), ())),
            preferred_element_type=jnp.float32,
        )
        page = grid_of((1, every), 1) // owned_pages
        sent = (owner_row == me.astype(jnp.float32)) & (page == i)
        number = jnp.sum(jnp.where(sent, 1.0, 0.0), 1, keepdims=True)
        slot = grid_of((1, CAP * PAGE), 1) // PAGE
        ok = (slot == grid_of((each, 1), 0) % CAP) & (slot.astype(jnp.float32) < number)
        scores = jnp.where(ok, scores * scale, -1e30)
        old_top = near_max[rows, :]
        top = jnp.maximum(jnp.max(scores, 1, keepdims=True), old_top)
        weights = jnp.where(ok, jnp.exp(scores - top), 0.0)
        keep = jnp.exp(old_top - top)
        total = near_sum[rows, :] * keep + jnp.sum(weights, 1, keepdims=True)
        mixed = jnp.dot(
            weights.astype(jnp.bfloat16), rbuf[h, i], preferred_element_type=jnp.float32
        )
        final = (near_out[rows, :] * keep + mixed) / total
        for j in range(share):
            at_col = (h * share + j) * HD
            result[i * CAP : (i + 1) * CAP, at_col : at_col + HD] = final[
                j * CAP : (j + 1) * CAP, :
            ]

    def finish(h):
        for ph in (h, kv_heads + h):
            for step in range(1, n_group):
                page_wait(ph, step)
        for i in range(n_group):
            fresh(i, h)
        span = slice(h * share * HD, (h + 1) * share * HD)
        out_ref[:, span] = result[:, span].astype(jnp.bfloat16)

    half = count // 2

    def multiply(ph, index):
        span = pl.ds(pl.multiple_of(index * depth, depth), depth)

        @pl.loop(0, 2)
        def _(i):
            rows = pl.ds(pl.multiple_of(i * half, half), half)
            acc[ph, rows, :] += jnp.dot(
                tok[rows, span], wbuf[ph, index], preferred_element_type=jnp.float32
            )

    per_owner = slots // n_group

    def page_copy(ph, step):
        to = lax.rem(me + step, n_group)
        return send(
            obuf.at[ph, to], rbuf.at[ph, me], page_send.at[ph, to], page_recv.at[ph, me], to
        )

    def page_wait(ph, step):
        origin = lax.rem(me + step, n_group)
        send(
            obuf.at[ph, origin],
            rbuf.at[ph, origin],
            page_send.at[ph, origin],
            page_recv.at[ph, origin],
            origin,
        ).wait_recv()

    def hand_over(ph):
        held = acc[ph]
        if ph >= kv_heads:
            held = held * cos_ref[...] + pltpu.roll(held, HD // 2, 1) * sin_ref[...]
        held = held.astype(jnp.bfloat16)

        for owner in range(n_group):
            rows = choose[owner * per_owner : (owner + 1) * per_owner, :]
            picked = jnp.dot(rows, held, preferred_element_type=jnp.float32)
            obuf[ph, owner] = picked.astype(jnp.bfloat16)
        for step in range(1, n_group):
            page_copy(ph, step).start()
        rbuf[ph, me] = obuf[ph, me]

    def at(step, way):
        ph = lax.div(step, line)
        dist = lax.rem(step, line)
        zz = z + dist * (2 * way - 1)
        live = (zz >= 0) & (zz < line) & ((dist > 0) | (way == 0))
        return ph, dist, zz, live

    def forward(ph, dist, zz, way, copy):
        @pl.when((way == 0) & (z < line - 1))
        def _():
            copy(ph, zz, True).start()

        @pl.when((way == 1) & (z > 0))
        def _():
            copy(ph, zz, False).start()

    @pl.loop(0, phases * line + PEER_LAG)
    def _(step):
        @pl.when(step < phases * line)
        def _():
            @pl.loop(0, 2)
            def _(way):
                ph, dist, zz, live = at(step, way)

                @pl.when(live & (dist > 0))
                def _():
                    main_copy(ph, zz, True).wait_recv()
                    forward(ph, dist, zz, way, main_copy)
                    xhead_copy(ph, zz, x).start()

            following = lax.div(step, line) + 1

            @pl.when((lax.rem(step, line) == 1) & (following + 1 < phases))
            def _():
                start_own(following + 1)

            @pl.when((lax.rem(step, line) == 2) & (following < phases))
            def _():
                pass_own_tail(following)

            @pl.loop(0, 2)
            def _(way):
                ph, dist, zz, live = at(step, way)

                @pl.when(live)
                def _():
                    multiply(ph, zz * 2 + x)

            @pl.when(step < n_group)
            def _():
                near(step)

        @pl.when((step >= TAIL_LAG) & (step < phases * line + TAIL_LAG))
        def _():
            @pl.loop(0, 2)
            def _(way):
                ph, dist, zz, live = at(step - TAIL_LAG, way)

                @pl.when(live & (dist > 0))
                def _():
                    tail_copy(ph, zz, True).wait_recv()
                    forward(ph, dist, zz, way, tail_copy)

        @pl.when(step >= PEER_LAG)
        def _():
            @pl.loop(0, 2)
            def _(way):
                ph, dist, zz, live = at(step - PEER_LAG, way)

                @pl.when(live)
                def _():
                    xhead_copy(ph, zz, peer_x).wait_recv()
                    multiply(ph, zz * 2 + peer_x)

        for ph in range(phases - 1):

            @pl.when(step == (ph + 1) * line + PEER_LAG - 1)
            def _():
                hand_over(ph)

    hand_over(phases - 1)
    for h in range(kv_heads):
        finish(h)

    for ph in range(phases):
        xtail_copy(ph, x).wait_send()
        for zz in range(line):
            xhead_copy(ph, zz, x).wait_send()

            @pl.when((z < line - 1) & (zz <= z))
            def _():
                main_copy(ph, zz, True).wait_send()
                tail_copy(ph, zz, True).wait_send()

            @pl.when((z > 0) & (zz >= z))
            def _():
                main_copy(ph, zz, False).wait_send()
                tail_copy(ph, zz, False).wait_send()

        for step in range(1, n_group):
            page_copy(ph, step).wait_send()


def per_device_fused(
    tokens, norm_gain, w_key, w_value, positions, page_owner, queries, kv_cache, cache_lengths
):
    count, width = tokens.shape
    depth, cols = w_key.shape
    n_group = lax.axis_size("group")
    line = n_group // 2
    slots = n_group * CAP * PAGE
    cut = depth - depth * 3 // 32
    phases = 2 * cols // HD
    rows = queries.shape[0]
    asked = rows * queries.shape[1] // HD
    cache = kv_cache.reshape(-1, HD)
    vmem = pl.BlockSpec(memory_space=pltpu.VMEM)
    hbm = pl.BlockSpec(memory_space=pl.ANY)
    dma = pltpu.SemaphoreType.DMA
    f32, bf16 = jnp.float32, jnp.bfloat16
    return pl.pallas_call(
        functools.partial(project_kernel, n_group, cut),
        out_shape=jax.ShapeDtypeStruct(queries.shape, bf16),
        in_specs=[hbm, vmem, hbm, hbm, vmem, vmem, vmem, hbm, vmem],
        out_specs=vmem,
        scratch_shapes=[
            pltpu.VMEM((count, width), bf16),
            pltpu.VMEM((phases, n_group, depth, HD), bf16),
            pltpu.VMEM((phases, count, HD), f32),
            pltpu.VMEM((slots, count), bf16),
            pltpu.VMEM((phases, n_group, slots // n_group, HD), bf16),
            pltpu.VMEM((phases, n_group, slots // n_group, HD), bf16),
            pltpu.VMEM((count, HD), f32),
            pltpu.VMEM((count, HD), f32),
            pltpu.VMEM(cache.shape, bf16),
            pltpu.VMEM(queries.shape, f32),
            pltpu.VMEM((asked, HD), bf16),
            pltpu.VMEM((asked, HD), f32),
            pltpu.VMEM((asked, HD), f32),
            pltpu.VMEM((asked, HD), f32),
            pltpu.VMEM(queries.shape, f32),
            dma,
            dma,
            dma((phases,)),
            dma((phases, line)),
            dma((phases, line)),
            dma((phases, line)),
            dma((phases, line)),
            dma((phases, line)),
            dma((phases, line)),
            dma((phases, line)),
            dma((phases,)),
            dma((phases, line)),
            dma((phases, n_group)),
            dma((phases, n_group)),
        ],
        compiler_params=pltpu.CompilerParams(
            collective_id=0, has_side_effects=True, vmem_limit_bytes=VMEM_BUDGET
        ),
        cost_estimate=pl.CostEstimate(
            flops=4 * count * width * cols,
            bytes_accessed=2 * count * width + 4 * depth * cols,
            transcendentals=0,
        ),
    )(
        tokens,
        norm_gain[None, :],
        w_key,
        w_value,
        positions[None, :],
        page_owner.reshape(1, -1),
        queries,
        cache,
        cache_lengths[None, :],
    )


def fits(count, width, cols, ngroup):
    slots = ngroup * CAP * PAGE
    held = 2 * count * width + 4 * width * cols + 8 * count * cols
    held += 2 * slots * count + 8 * slots * cols + 8 * count * HD
    return 3 * held < 2 * VMEM_BUDGET


def pick(tokens, norm_gain, w_key, *rest):
    ngroup = lax.axis_size("group")
    count, width = tokens.shape
    fused = ngroup >= 6 and ngroup % 2 == 0 and count % 256 == 0 and w_key.shape[0] % 1024 == 0
    fused = fused and fits(count, width, w_key.shape[1], ngroup)
    return (per_device_fused if fused else per_device)(tokens, norm_gain, w_key, *rest)


def solution(mesh):
    return jax.shard_map(
        pick,
        mesh=mesh,
        in_specs=(
            P("group", None),
            P(),
            P("group", "tensor"),
            P("group", "tensor"),
            P("group"),
            P(),
            P("group", "tensor"),
            P("group", None, None, "tensor", None),
            P("group"),
        ),
        out_specs=P("group", "tensor"),
        check_vma=False,
    )
```
